1024 devices in a mesh: gx: 32 (over y_lo, z), gy: 16 (over x, y_hi), gz: 2 (over core).
Axes of the slice: x: 8, y: 8 (y_hi: 2, y_lo: 4; y = y_hi * 4 + y_lo), z: 8, core: 2. Of those that a mesh axis runs over, the one named last changes fastest.
Arguments:
- electric: float32 [3, 256, 256, 96], P(None, 'gx', 'gy', 'gz'), may hold values from -6 to 6
- magnetic: float32 [3, 256, 256, 96], P(None, 'gx', 'gy', 'gz'), may hold values from -6 to 6
- material: int32 [256, 256, 96], P('gx', 'gy', 'gz'), may hold values from 0 to 3
- permittivity: float32 [4], replicated, may hold values from 1 to 12
- source_cells: int32 [64, 3], replicated, may hold values from 0 to 255, as said below
- amplitudes: float32 [64, 3], replicated, may hold values from -16 to 16
- omegas: float32 [4], replicated, may hold values from 0.3 to 1.5
- design_mask: int32 [256, 8192], P('gx', ('gy', 'gz')), may hold values 0 or 1
- forward_dft: float32 [256, 24, 8192], P('gx', None, ('gy', 'gz')), may hold values from -6 to 6
- pixel_anchor: int32 [3], replicated, may hold values from 0 to 2
Outputs:
- adjoint_dft: float32 [256, 24, 8192], P('gx', None, ('gy', 'gz'))
- pixel_gradient: float32 [256, 8192], P('gx', ('gy', 'gz'))
- final_electric: float32 [3, 256, 256, 96], P(None, 'gx', 'gy', 'gz')
The draws below stay inside these ranges and needn't reach their ends.
Inputs may be any that keep to these rules, and one draw needn't show every extreme that they name: `source_cells`: column 0 is below 256, column 1 below 256, column 2 below 96.
All inputs are finite; a program needn't handle non-finite values. No bound on the sum of `design_mask` on one device may be relied on, other than what follows from the above.
Results may differ from the reference program's by a relative error of at most 0.00011.
Values sent between devices are 32-bit elements; how exact they have to be, the bound alone decides.
A program may use at most 32 MiB of HBM per device.

```python
import math
import jax
import jax.numpy as jnp
from jax import lax

CZ = 48
SLAB = 32
FREQ = 4
ITERS = 2
MATS = 4
NSRC = 64
NX = 256
NY = 256
NZ = 96


def draw_source_cells(key, part):
    key_x, key_y, key_z = jax.random.split(key, 3)
    column_x = jax.random.randint(key_x, (NSRC,), 0, NX).astype(jnp.int32)
    column_y = jax.random.randint(key_y, (NSRC,), 0, NY).astype(jnp.int32)
    column_z = jax.random.randint(key_z, (NSRC,), 0, NZ).astype(jnp.int32)
    column_x = column_x.at[0].set(NX - 1).at[1].set(0)
    column_y = column_y.at[0].set(NY - 1).at[1].set(0)
    column_z = column_z.at[0].set(NZ - 1).at[1].set(0)
    return jnp.stack([column_x, column_y, column_z], axis=1).astype(jnp.int32)


def plant(result, stream_key, least, high):
    longest = result.shape.index(max(result.shape))
    spots = []
    for shift in (0, 1):
        where = [jax.random.randint(jax.random.fold_in(stream_key, axis), (), 0, length) for axis, length in enumerate(result.shape)]
        where[longest] = (where[longest] + shift) % result.shape[longest]
        spots.append(tuple(where))
    return result.at[spots[0]].set(least).at[spots[1]].set(high)


def levels(rng, extent, cuts, least, largest):
    def one(position, parts):
        heights = jax.random.uniform(jax.random.fold_in(jax.random.fold_in(rng, 6), position), (parts,), jnp.float32, least / len(cuts), largest / len(cuts))
        return jnp.repeat(jnp.exp(heights), extent[position] // parts).reshape((-1,) + (1,) * (len(extent) - position - 1))

    level = one(*cuts[0])
    for cut in cuts[1:]:
        level = level * one(*cut)
    return level


def scatter_about(rng, extent, width, most, cuts=(), held_as=jnp.bfloat16):
    values = width * jax.random.normal(rng, extent, jnp.float32)
    if cuts:
        values = values * levels(rng, extent, cuts, -0.22, 0.18)
    return jnp.clip(values, -most, most).astype(held_as)


def setup_inputs(seed: int = 0) -> dict:
    streams_of = jax.random.split(jax.random.key(seed), 11)
    electric = scatter_about(streams_of[0], (3, NX, NY, NZ), 1.0, 6.0, ((1, 32), (2, 16), (3, 2)), jnp.float32)
    magnetic = scatter_about(streams_of[1], (3, NX, NY, NZ), 1.0, 6.0, ((1, 32), (2, 16), (3, 2)), jnp.float32)
    material = plant(jax.random.randint(streams_of[2], (NX, NY, NZ), 0, MATS), jax.random.fold_in(streams_of[2], 1), 0, MATS - 1).astype(jnp.int32)
    permittivity = jnp.clip(jax.random.uniform(streams_of[3], (MATS,), jnp.float32, 1.0, 12.0), 1.0, 12.0)
    source_cells = draw_source_cells(jax.random.fold_in(streams_of[10], 71), 0)
    amplitudes = scatter_about(streams_of[5], (NSRC, 3), 4.0, 16.0, (), jnp.float32)
    omegas = jnp.clip(jax.random.uniform(streams_of[6], (FREQ,), jnp.float32, 0.3, 1.5), 0.3, 1.5)
    design_mask = plant((jax.random.randint(streams_of[7], (NX, NY * SLAB), 0, 4) < 3).astype(jnp.int32), jax.random.fold_in(streams_of[7], 1), 0, 1)
    forward_dft = scatter_about(streams_of[8], (NX, 6 * FREQ, NY * SLAB), 1.0, 6.0, ((0, 32), (2, 32)), jnp.float32)
    pixel_anchor = jax.random.randint(streams_of[9], (3,), 0, 3).astype(jnp.int32)
    return dict(electric=electric, magnetic=magnetic, material=material, permittivity=permittivity, source_cells=source_cells, amplitudes=amplitudes, omegas=omegas, design_mask=design_mask, forward_dft=forward_dft, pixel_anchor=pixel_anchor)


COURANT = 0.5


def forward_diff(grid_field, direction):
    length = grid_field.shape[direction]
    following = jnp.concatenate([lax.slice_in_dim(grid_field, 1, length, axis=direction), jnp.zeros_like(lax.slice_in_dim(grid_field, 0, 1, axis=direction))], axis=direction)
    return following - grid_field


def backward_diff(grid_field, direction):
    length = grid_field.shape[direction]
    previous = jnp.concatenate([jnp.zeros_like(lax.slice_in_dim(grid_field, 0, 1, axis=direction)), lax.slice_in_dim(grid_field, 0, length - 1, axis=direction)], axis=direction)
    return grid_field - previous


def magnetic_step(electric, magnetic):
    curl_x = forward_diff(electric[2], 1) - forward_diff(electric[1], 2)
    curl_y = forward_diff(electric[0], 2) - forward_diff(electric[2], 0)
    curl_z = forward_diff(electric[1], 0) - forward_diff(electric[0], 1)
    return magnetic - COURANT * jnp.stack([curl_x, curl_y, curl_z])


def electric_step(electric, magnetic, coefficient, source_term):
    curl_x = backward_diff(magnetic[2], 1) - backward_diff(magnetic[1], 2)
    curl_y = backward_diff(magnetic[0], 2) - backward_diff(magnetic[2], 0)
    curl_z = backward_diff(magnetic[1], 0) - backward_diff(magnetic[0], 1)
    return electric + coefficient * (jnp.stack([curl_x, curl_y, curl_z]) - source_term)


def spectral_weights(omegas, step_index):
    phases = omegas * (step_index + 1)
    return jnp.stack([jnp.cos(phases), -jnp.sin(phases)])


def accumulate(running, weights, slab_field):
    return running + weights[:, :, None, None, None, None] * slab_field[None, None]


def sensitivity(forward_dft, adjoint_dft, omegas, design_mask):
    product = (forward_dft * adjoint_dft).reshape(forward_dft.shape[0], 2, FREQ, 3, forward_dft.shape[2])
    real_part = jnp.sum(product[:, 0] - product[:, 1], axis=2)
    return 0.05 * jnp.sum((omegas * omegas)[None, :, None] * real_part, axis=1) * design_mask.astype(jnp.float32)


def pixel_fold(padded, coords, offset, direction):
    length = padded.shape[direction] - 4
    view_shape = [1] * padded.ndim
    view_shape[direction] = length
    home_pixel = (coords + offset) // 3
    running = lax.slice_in_dim(padded, 2, 2 + length, axis=direction)
    for displacement in (-2, -1, 1, 2):
        neighbor = lax.slice_in_dim(padded, 2 + displacement, 2 + displacement + length, axis=direction)
        same_pixel = ((coords + displacement + offset) // 3 == home_pixel).reshape(view_shape)
        running = running + jnp.where(same_pixel, neighbor, 0.0)
    return running


def reference(electric, magnetic, material, permittivity, source_cells, amplitudes, omegas, design_mask, forward_dft, pixel_anchor):
    coefficient = COURANT / permittivity[material]
    source_field = jnp.zeros_like(electric).at[:, source_cells[:, 0], source_cells[:, 1], source_cells[:, 2]].add(amplitudes.T)
    bottom = CZ // 4
    spectrum = jnp.zeros((2, FREQ, 3, NX, NY, SLAB), jnp.float32)
    for step_index in range(ITERS):
        magnetic = magnetic_step(electric, magnetic)
        electric = electric_step(electric, magnetic, coefficient, source_field * math.cos(0.7 * (step_index + 0.5)))
        spectrum = accumulate(spectrum, spectral_weights(omegas, step_index), electric[:, :, :, bottom:bottom + SLAB])
    adjoint_dft = jnp.transpose(spectrum, (3, 0, 1, 2, 4, 5)).reshape(NX, 6 * FREQ, NY * SLAB)
    gradient = sensitivity(forward_dft, adjoint_dft, omegas, design_mask).reshape(NX, NY, SLAB)
    gradient = pixel_fold(jnp.pad(gradient, ((2, 2), (0, 0), (0, 0))), jnp.arange(NX, dtype=jnp.int32), pixel_anchor[0], 0)
    gradient = pixel_fold(jnp.pad(gradient, ((0, 0), (2, 2), (0, 0))), jnp.arange(NY, dtype=jnp.int32), pixel_anchor[1], 1)
    gradient = pixel_fold(jnp.pad(gradient, ((0, 0), (0, 0), (2, 2))), jnp.arange(SLAB, dtype=jnp.int32), pixel_anchor[2], 2)
    return adjoint_dft, gradient.reshape(NX, NY * SLAB), electric
```

```python
import math

import jax
import jax.numpy as jnp
from jax import lax
from jax.experimental import pallas as pl
from jax.experimental.pallas import tpu as pltpu
from jax.sharding import PartitionSpec as P

SLAB = 32
FREQ = 4
MATS = 4
COURANT = 0.5

BX, BY, CZ = 8, 16, 48
HY = BY // 2
LANES = 128
DEPTH = 2 * CZ
BOTTOM = CZ // 4
COMPS = 7
ROWS = COMPS * BX
PAIRS = BY // 2
SENT = 5
YY = 12
SUB = 16


def roll(v, by, axis):
    return pltpu.roll(v, by % v.shape[axis], axis)


def iota(shape, axis):
    return lax.broadcasted_iota(jnp.int32, shape, axis)


def third(v):
    return (v * 21846) >> 16


def same_pixel(coord, anchor, by):
    shifted = coord + anchor
    place = shifted - 3 * third(shifted) + by
    return (place >= 0) & (place <= 2)


def kernel(
    e_in, h_in, mat_in, perm, cells_in, amps_in, omegas, mask_in, fwd_in, anchor,
    adj, grad, fe,
    e_v, h_v, mat_v, cells_v, amps_v, mask_v, fwd_v, adj_v, coef_v,
    packed, edge, body, halo, merged, fields, source, flat,
    fe_send, fe_recv, g_send, g_x, g_y, g_c,
    load_sem, send_sem, recv_sem,
):
    nx, ny = lax.axis_size("gx"), lax.axis_size("gy")
    gx, gy, core = lax.axis_index("gx"), lax.axis_index("gy"), lax.axis_index("gz")
    other = 1 - core
    up_x, down_x = lax.rem(gx + 1, nx), lax.rem(gx + nx - 1, nx)
    up_y, down_y = lax.rem(gy + 1, ny), lax.rem(gy + ny - 1, ny)

    barrier = pltpu.get_barrier_semaphore()
    face_y = jnp.where(core == 0, down_y, up_y)
    senders = [(gx, gy, other)]
    for h in (0, 1):
        senders += [(up_x, gy, h), (down_x, gy, h)]
        senders += [(gx, face_y, h), (up_x, face_y, h), (down_x, face_y, h)]
    for sender in senders:
        pl.semaphore_signal(barrier, inc=1, device_id=sender, device_id_type=pl.DeviceIdType.MESH)

    loads = [
        pltpu.make_async_copy(src, dst, load_sem.at[i])
        for i, (src, dst) in enumerate(
            [(mat_in, mat_v), (e_in, e_v), (h_in, h_v), (cells_in, cells_v), (amps_in, amps_v),
             (mask_in, mask_v)]
            + [(fwd_in.at[:, pl.ds(LANES * t, LANES)], fwd_v.at[t]) for t in (0, 1)]
        )
    ]
    for load in loads:
        load.start()

    edge[...] = jnp.zeros_like(edge)
    halo[:, :, 16:48, :] = jnp.zeros((2, YY // 2, 32, LANES), jnp.float32)

    for load in loads[:3]:
        load.wait()
    material = mat_v[...]
    eps = jnp.zeros(material.shape, jnp.float32)
    for level in range(MATS):
        eps = eps + jnp.where(material == level, perm[level], 0.0)
    coef_v[...] = COURANT / eps
    blank = jnp.zeros((ROWS, LANES - DEPTH), jnp.float32)
    for pair in range(PAIRS):
        rows = [
            jnp.concatenate(
                [
                    e_v[pl.ds(y, 3 * BX, stride=BY), :],
                    h_v[pl.ds(y, 3 * BX, stride=BY), :],
                    coef_v[pl.ds(y, BX, stride=BY), :],
                ],
                axis=0,
            )
            for y in (2 * pair, 2 * pair + 1)
        ]
        packed[pair] = jnp.concatenate(rows + [blank], axis=1)
    for pair in range(PAIRS):
        for side, first in ((0, 0), (1, BX - 2)):
            for x in (0, 1):
                edge[side, pair, pl.ds(8 * x, COMPS), :] = packed[
                    pair, pl.ds(first + x, COMPS, stride=BX), :
                ]

    def remote(src, dst, role, device):
        return pltpu.make_async_remote_copy(
            src_ref=src,
            dst_ref=dst,
            send_sem=send_sem.at[role[0]],
            recv_sem=recv_sem.at[role[1]],
            device_id=device,
            device_id_type=pl.DeviceIdType.MESH,
        )

    def part(dest):
        return packed.at[pl.ds(3 * dest, SENT)]

    def part_edge(side, dest):
        return edge.at[side, pl.ds(3 * dest, SENT)]

    def span(dest):
        return pl.ds(1 - dest, SENT)

    pl.semaphore_wait(barrier, len(senders))
    sends = [
        remote(packed.at[PAIRS - 1], body.at[core, 0], (1, 1 + core), (gx, up_y, 0)),
        remote(packed.at[0], body.at[core, 5], (2, 1 + core), (gx, down_y, 1)),
    ]
    for side, to_x in ((0, down_x), (1, up_x)):
        place = pl.ds(48 * side, 16)
        sends += [
            remote(edge.at[side, PAIRS - 1], halo.at[core, 0, place], (3 + 4 * side, 7 + 2 * side + core), (to_x, up_y, 0)),
            remote(edge.at[side, 0], halo.at[core, 5, place], (4 + 4 * side, 7 + 2 * side + core), (to_x, down_y, 1)),
        ]
    for side, to_x in ((0, down_x), (1, up_x)):
        place = pl.ds(48 * side, 16)
        for dest in (0, 1):
            sends.append(
                remote(part_edge(side, dest), halo.at[core, span(dest), place], (5 + 4 * side + dest, 3 + 2 * side + core), (to_x, gy, dest))
            )
    sends.append(remote(part(other), body.at[core, span(other)], (0, 0), (gx, gy, other)))
    for send in sends:
        send.start()

    body[core, span(core)] = packed[pl.ds(3 * core, SENT)]
    for load in loads[3:]:
        load.wait()

    y_first = gy * BY + core * HY - 2
    row = iota((YY * SUB, 64), 0)
    sub = row & (SUB - 1)
    row_x = gx * BX + jnp.where(sub < 12, sub, sub - SUB)
    row_y = y_first + (row >> 4)
    hit = (row_x == cells_v[0:1, :]) & (row_y == cells_v[1:2, :])
    hit_z = jnp.where(iota((LANES, 64), 0) == cells_v[2:3, :], 1.0, 0.0)
    for c in range(3):
        left = jnp.where(hit, amps_v[c : c + 1, :], 0.0)
        source[c] = lax.dot_general(
            left, hit_z, (((1,), (1,)), ((), ())),
            precision=lax.Precision.HIGHEST, preferred_element_type=jnp.float32,
        ).reshape(YY, SUB, LANES)

    shape = (BX, LANES)
    r = iota(shape, 0)
    omega = jnp.zeros(shape, jnp.float32)
    for f in range(FREQ):
        omega = jnp.where((r & 3) == f, omegas[f], omega)
    phase = omega * ((r >> 2) + 1).astype(jnp.float32)
    cosine = jnp.cos(phase)
    sine = -jnp.sin(phase)
    square = omega * omega

    face = 1 - core
    y_in = jnp.where(core == 0, gy > 0, gy < ny - 1)

    remote(part(core), body.at[other, span(core)], (0, 0), (gx, gy, other)).wait_recv()
    for h in (0, 1):
        remote(packed.at[0], body.at[h, 5 * core], (0, 1 + h), (gx, gy, other)).wait_recv()
        for side in (0, 1):
            place = pl.ds(48 * side, 16)
            remote(edge.at[0, pl.ds(0, SENT)], halo.at[h, span(core), place], (0, 3 + 2 * side + h), (gx, gy, other)).wait_recv()
            remote(edge.at[0, 0], halo.at[h, 5 * core, place], (0, 7 + 2 * side + h), (gx, gy, other)).wait_recv()

    x_of = iota((SUB, LANES), 0)
    x_of = gx * BX + jnp.where(x_of < 12, x_of, x_of - SUB)
    lane = iota((SUB, LANES), 1)
    inside = (x_of >= 0) & (x_of < nx * BX) & (lane < DEPTH)
    y_end = ny * BY

    lane_b = iota((ROWS, LANES), 1)
    lane_h = iota((64, LANES), 1)

    def merge(low, high, lanes):
        even = jnp.where(lanes < CZ, low, roll(high, CZ, 1))
        odd = jnp.where(lanes < CZ, roll(low, -CZ, 1), high)
        return even, odd

    for pair in range(YY // 2):
        own = merge(body[0, pair], body[1, pair], lane_b)
        beside = merge(halo[0, pair], halo[1, pair], lane_h)
        for k in (0, 1):
            merged[k] = beside[k]
            yy = 2 * pair + k
            y = y_first + yy
            ok = inside & (y >= 0) & (y < y_end)
            for j in range(COMPS):
                tile = jnp.concatenate([own[k][BX * j : BX * j + BX], merged[k, pl.ds(j, 8, stride=8), :]], axis=0)
                fields[j, yy] = jnp.where(ok, tile, 0.0)

    half = jnp.where(inside, COURANT, 0.0)

    def magnetic_rows(first, last):
        def step(yy, carry):
            e0, e1, e2 = fields[0, yy], fields[1, yy], fields[2, yy]
            n0, n2 = fields[0, yy + 1], fields[2, yy + 1]
            y = y_first + yy
            scale = jnp.where((y >= 0) & (y < y_end), half, 0.0)
            fields[3, yy] = fields[3, yy] - scale * ((n2 - e2) - (roll(e1, -1, 1) - e1))
            fields[4, yy] = fields[4, yy] - scale * ((roll(e0, -1, 1) - e0) - (roll(e2, -1, 0) - e2))
            fields[5, yy] = fields[5, yy] - scale * ((roll(e1, -1, 0) - e1) - (n0 - e0))
            return carry

        lax.fori_loop(first, last, step, 0, unroll=True)

    def electric_rows(first, last, time):
        factor = math.cos(0.7 * (time + 0.5))

        def step(yy, carry):
            h0, h1, h2 = fields[3, yy], fields[4, yy], fields[5, yy]
            p0, p2 = fields[3, yy - 1], fields[5, yy - 1]
            scale = fields[6, yy]
            curls = (
                (h2 - p2) - (h1 - roll(h1, 1, 1)),
                (h0 - roll(h0, 1, 1)) - (h2 - roll(h2, 1, 0)),
                (h1 - roll(h1, 1, 0)) - (h0 - p0),
            )
            for c in range(3):
                fields[c, yy] = fields[c, yy] + scale * (curls[c] - factor * source[c, yy])
            return carry

        lax.fori_loop(first, last, step, 0, unroll=True)

    quarter = iota((BX, LANES), 1) >> 5

    def flatten(time):
        for c in range(3):
            for tile in (0, 1):
                out = jnp.zeros((BX, LANES), jnp.float32)
                for q in range(4):
                    v = fields[c, 2 + 4 * tile + q, 0:BX, :]
                    out = jnp.where(quarter == q, roll(v, SLAB * q - BOTTOM, 1), out)
                flat[time, c, :, pl.ds(LANES * tile, LANES)] = out

    magnetic_rows(0, 11)
    electric_rows(1, 11, 0)
    flatten(0)
    magnetic_rows(1, 10)
    electric_rows(2, 10, 1)
    flatten(1)

    for y in range(HY):
        v = jnp.concatenate([fields[c, 2 + y, 0:BX, :] for c in range(3)], axis=0)
        moved = roll(v, -CZ, 1)
        first = core == 0
        fe[pl.ds(HY * core + y, 3 * BX, stride=BY), :] = jnp.where(first, v, moved)[:, :CZ]
        fe_send[y] = jnp.where(first, moved, v)
    fe_copy = remote(fe_send, fe_recv, (11, 11), (gx, gy, other))
    fe_copy.start()

    totals = []
    for t in (0, 1):
        lanes = pl.ds(LANES * t, LANES)
        total = jnp.zeros((BX, LANES), jnp.float32)
        for f in range(FREQ):
            real = jnp.zeros((BX, LANES), jnp.float32)
            for p, weights in ((0, cosine), (1, sine)):
                for c in range(3):
                    rows = pl.ds(3 * FREQ * p + 3 * f + c, BX, stride=6 * FREQ)
                    value = weights[f : f + 1, :] * flat[0, c, :, lanes] + weights[4 + f : 5 + f, :] * flat[1, c, :, lanes]
                    adj_v[t, rows, :] = value
                    product = fwd_v[t, rows, :] * value
                    real = real + product if p == 0 else real - product
            total = total + square[f : f + 1, :] * real
        totals.append(total)
    stores = [
        pltpu.make_async_copy(adj_v.at[t], adj.at[:, pl.ds(LANES * t, LANES)], load_sem.at[8 + t]) for t in (0, 1)
    ]
    for store in stores:
        store.start()
    total = 0.05 * jnp.concatenate(totals, axis=1) * mask_v[...].astype(jnp.float32)

    shape = (BX, 2 * LANES)
    z = iota(shape, 1) & (SLAB - 1)
    folded = total
    for by in (-2, -1, 1, 2):
        ok = same_pixel(z, anchor[2], by) & (z + by >= 0) & (z + by < SLAB)
        folded = folded + jnp.where(ok, roll(total, -by, 1), 0.0)
    g_send[...] = folded

    above = (gx, jnp.where(core == 0, gy, up_y), other)
    below = (gx, jnp.where(core == 0, down_y, gy), other)
    first_rows, last_rows = g_send.at[:, pl.ds(0, LANES)], g_send.at[:, pl.ds(LANES, LANES)]
    swaps = [
        remote(first_rows, g_y.at[0], (12, 12), below),
        remote(last_rows, g_y.at[1], (13, 13), above),
        remote(first_rows, g_c.at[0, 0], (14, 14), (down_x,) + below[1:]),
        remote(last_rows, g_c.at[0, 1], (15, 15), (down_x,) + above[1:]),
        remote(first_rows, g_c.at[1, 0], (16, 16), (up_x,) + below[1:]),
        remote(last_rows, g_c.at[1, 1], (17, 17), (up_x,) + above[1:]),
        remote(g_send, g_x.at[0], (18, 18), (down_x, gy, core)),
        remote(g_send, g_x.at[1], (19, 19), (up_x, gy, core)),
    ]
    for swap in swaps:
        swap.start()

    fe_copy.wait_recv()
    for y in range(HY):
        fe[pl.ds(HY * other + y, 3 * BX, stride=BY), :] = fe_recv[y][:, :CZ]

    for swap in swaps:
        swap.wait_recv()
    block = gy * 2 + core
    wide = (BX, 4 * LANES)
    tile0 = jnp.concatenate([folded, g_y[0], g_y[1]], axis=1)
    upper = jnp.concatenate([g_x[0], g_c[0, 0], g_c[0, 1]], axis=1)
    lower = jnp.concatenate([g_x[1], g_c[1, 0], g_c[1, 1]], axis=1)
    x_row, column = iota(wide, 0), iota(wide, 1)
    upper = jnp.where(gx < nx - 1, upper, 0.0)
    lower = jnp.where(gx > 0, lower, 0.0)
    tile1 = jnp.where(x_row < 4, upper, lower)
    y_ok = (column < 2 * LANES) | ((column < 3 * LANES) & (block < 2 * ny - 1)) | ((column >= 3 * LANES) & (block > 0))
    extended = jnp.where(
        jnp.concatenate([y_ok, y_ok], axis=0), jnp.concatenate([tile0, tile1], axis=0), 0.0
    )
    along_x = extended[:BX]
    for by in (-2, -1, 1, 2):
        ok = same_pixel(gx * BX + x_row, anchor[0], by)
        along_x = along_x + jnp.where(ok, roll(extended, -by, 0)[:BX], 0.0)
    result = along_x[:, : 2 * LANES]
    y_row = block * HY + (iota(shape, 1) >> 5)
    for by in (-2, -1, 1, 2):
        ok = same_pixel(y_row, anchor[1], by)
        result = result + jnp.where(ok, roll(along_x, -SLAB * by, 1)[:, : 2 * LANES], 0.0)
    grad[...] = result

    for send in sends + [fe_copy] + swaps:
        send.wait_send()
    for store in stores:
        store.wait()


def body_fn(
    electric, magnetic, material, permittivity, source_cells, amplitudes, omegas, design_mask, forward_dft, pixel_anchor
):
    f32 = jnp.float32
    anywhere = pl.BlockSpec(memory_space=pl.ANY)
    scalars = pl.BlockSpec(memory_space=pltpu.SMEM)
    vmem = pl.BlockSpec(memory_space=pltpu.VMEM)
    adj, grad, fe = pl.pallas_call(
        kernel,
        out_shape=(
            jax.ShapeDtypeStruct((BX * 6 * FREQ, 2 * LANES), f32),
            jax.ShapeDtypeStruct((BX, 2 * LANES), f32),
            jax.ShapeDtypeStruct((3 * BX * BY, CZ), f32),
        ),
        in_specs=[anywhere, anywhere, anywhere, scalars, anywhere, anywhere, scalars, anywhere, anywhere, scalars],
        out_specs=(anywhere, vmem, vmem),
        scratch_shapes=[
            pltpu.VMEM((3 * BX * BY, CZ), f32),
            pltpu.VMEM((3 * BX * BY, CZ), f32),
            pltpu.VMEM((BX * BY, CZ), jnp.int32),
            pltpu.VMEM((3, 64), jnp.int32),
            pltpu.VMEM((3, 64), f32),
            pltpu.VMEM((BX, 2 * LANES), jnp.int32),
            pltpu.VMEM((2, BX * 6 * FREQ, LANES), f32),
            pltpu.VMEM((2, BX * 6 * FREQ, LANES), f32),
            pltpu.VMEM((BX * BY, CZ), f32),
            pltpu.VMEM((PAIRS, ROWS, LANES), f32),
            pltpu.VMEM((2, PAIRS, 16, LANES), f32),
            pltpu.VMEM((2, YY // 2, ROWS, LANES), f32),
            pltpu.VMEM((2, YY // 2, 64, LANES), f32),
            pltpu.VMEM((2, 64, LANES), f32),
            pltpu.VMEM((COMPS, YY, SUB, LANES), f32),
            pltpu.VMEM((3, YY, SUB, LANES), f32),
            pltpu.VMEM((2, 3, BX, 2 * LANES), f32),
            pltpu.VMEM((HY, 3 * BX, LANES), f32),
            pltpu.VMEM((HY, 3 * BX, LANES), f32),
            pltpu.VMEM((BX, 2 * LANES), f32),
            pltpu.VMEM((2, BX, 2 * LANES), f32),
            pltpu.VMEM((2, BX, LANES), f32),
            pltpu.VMEM((2, 2, BX, LANES), f32),
            pltpu.SemaphoreType.DMA((10,)),
            pltpu.SemaphoreType.DMA((20,)),
            pltpu.SemaphoreType.DMA((20,)),
        ],
        compiler_params=pltpu.CompilerParams(
            collective_id=0, has_side_effects=True, vmem_limit_bytes=24 * 1024 * 1024
        ),
    )(
        electric.reshape(3 * BX * BY, CZ),
        magnetic.reshape(3 * BX * BY, CZ),
        material.reshape(BX * BY, CZ),
        permittivity,
        source_cells.T,
        amplitudes.T,
        omegas,
        design_mask,
        forward_dft.reshape(BX * 6 * FREQ, 2 * LANES),
        pixel_anchor,
    )
    return adj.reshape(BX, 6 * FREQ, 2 * LANES), grad, fe.reshape(3, BX, BY, CZ)


def solution(mesh):
    return jax.shard_map(
        body_fn,
        mesh=mesh,
        in_specs=(
            P(None, "gx", "gy", "gz"),
            P(None, "gx", "gy", "gz"),
            P("gx", "gy", "gz"),
            P(),
            P(),
            P(),
            P(),
            P("gx", ("gy", "gz")),
            P("gx", None, ("gy", "gz")),
            P(),
        ),
        out_specs=(P("gx", None, ("gy", "gz")), P("gx", ("gy", "gz")), P(None, "gx", "gy", "gz")),
        check_vma=False,
    )
```

```python
import math

import jax
import jax.numpy as jnp
from jax import lax
from jax.experimental import pallas as pl
from jax.experimental.pallas import tpu as pltpu
from jax.sharding import PartitionSpec as P

SLAB = 32
FREQ = 4
MATS = 4
COURANT = 0.5

BX, BY, CZ = 8, 16, 48
HY = BY // 2
LANES = 128
DEPTH = 2 * CZ
BOTTOM = CZ // 4
COMPS = 7
ROWS = COMPS * BX
PAIRS = BY // 2
SENT = 5
YY = 12
SUB = 16


def roll(v, by, axis):
    return pltpu.roll(v, by % v.shape[axis], axis)


def iota(shape, axis):
    return lax.broadcasted_iota(jnp.int32, shape, axis)


def third(v):
    return (v * 21846) >> 16


def same_pixel(coord, anchor, by):
    shifted = coord + anchor
    place = shifted - 3 * third(shifted) + by
    return (place >= 0) & (place <= 2)


def kernel(
    e_in, h_in, mat_in, perm_in, cells_in, amps_in, omegas_in, mask_in, fwd_in, anchor_in,
    adj, grad, fe,
    perm, omegas, anchor,
    e_v, h_v, mat_v, cells_v, amps_v, mask_v, fwd_v, adj_v, coef_v,
    packed, edge, body, halo, merged, fields, source, gain, flat,
    fe_send, fe_recv, g_send, g_x, g_y, g_c,
    load_sem, send_sem, recv_sem,
):
    nx, ny = lax.axis_size("gx"), lax.axis_size("gy")
    gx, gy, core = lax.axis_index("gx"), lax.axis_index("gy"), lax.axis_index("gz")
    other = 1 - core
    up_x, down_x = lax.rem(gx + 1, nx), lax.rem(gx + nx - 1, nx)
    up_y, down_y = lax.rem(gy + 1, ny), lax.rem(gy + ny - 1, ny)

    barrier = pltpu.get_barrier_semaphore()
    face_y = jnp.where(core == 0, down_y, up_y)
    senders = [(gx, gy, other)]
    for h in (0, 1):
        senders += [(up_x, gy, h), (down_x, gy, h)]
        senders += [(gx, face_y, h), (up_x, face_y, h), (down_x, face_y, h)]
    for sender in senders:
        pl.semaphore_signal(barrier, inc=1, device_id=sender, device_id_type=pl.DeviceIdType.MESH)

    loads = [
        pltpu.make_async_copy(src, dst, load_sem.at[i])
        for i, (src, dst) in enumerate(
            [(perm_in, perm), (mat_in, mat_v), (e_in, e_v), (h_in, h_v), (cells_in, cells_v), (amps_in, amps_v),
             (omegas_in, omegas), (anchor_in, anchor), (mask_in, mask_v)]
            + [(fwd_in.at[:, pl.ds(LANES * t, LANES)], fwd_v.at[t]) for t in (0, 1)]
        )
    ]
    for load in loads:
        load.start()

    edge[...] = jnp.zeros_like(edge)
    halo[:, :, 16:48, :] = jnp.zeros((2, YY // 2, 32, LANES), jnp.float32)

    for load in loads[:4]:
        load.wait()
    material = mat_v[...]
    eps = jnp.zeros(material.shape, jnp.float32)
    for level in range(MATS):
        eps = eps + jnp.where(material == level, perm[level], 0.0)
    coef_v[...] = COURANT / eps
    blank = jnp.zeros((ROWS, LANES - DEPTH), jnp.float32)
    for pair in range(PAIRS):
        rows = [
            jnp.concatenate(
                [
                    e_v[pl.ds(y, 3 * BX, stride=BY), :],
                    h_v[pl.ds(y, 3 * BX, stride=BY), :],
                    coef_v[pl.ds(y, BX, stride=BY), :],
                ],
                axis=0,
            )
            for y in (2 * pair, 2 * pair + 1)
        ]
        packed[pair] = jnp.concatenate(rows + [blank], axis=1)
    for pair in range(PAIRS):
        for side, first in ((0, 0), (1, BX - 2)):
            for x in (0, 1):
                edge[side, pair, pl.ds(8 * x, COMPS), :] = packed[
                    pair, pl.ds(first + x, COMPS, stride=BX), :
                ]

    def remote(src, dst, role, device):
        return pltpu.make_async_remote_copy(
            src_ref=src,
            dst_ref=dst,
            send_sem=send_sem.at[role[0]],
            recv_sem=recv_sem.at[role[1]],
            device_id=device,
            device_id_type=pl.DeviceIdType.MESH,
        )

    def part(dest):
        return packed.at[pl.ds(3 * dest, SENT)]

    def part_edge(side, dest):
        return edge.at[side, pl.ds(3 * dest, SENT)]

    def span(dest):
        return pl.ds(1 - dest, SENT)

    pl.semaphore_wait(barrier, len(senders))
    sends = [
        remote(packed.at[PAIRS - 1], body.at[core, 0], (1, 1 + core), (gx, up_y, 0)),
        remote(packed.at[0], body.at[core, 5], (2, 1 + core), (gx, down_y, 1)),
    ]
    for side, to_x in ((0, down_x), (1, up_x)):
        place = pl.ds(48 * side, 16)
        sends += [
            remote(edge.at[side, PAIRS - 1], halo.at[core, 0, place], (3 + 4 * side, 7 + 2 * side + core), (to_x, up_y, 0)),
            remote(edge.at[side, 0], halo.at[core, 5, place], (4 + 4 * side, 7 + 2 * side + core), (to_x, down_y, 1)),
        ]
    for side, to_x in ((0, down_x), (1, up_x)):
        place = pl.ds(48 * side, 16)
        for dest in (0, 1):
            sends.append(
                remote(part_edge(side, dest), halo.at[core, span(dest), place], (5 + 4 * side + dest, 3 + 2 * side + core), (to_x, gy, dest))
            )
    sends.append(remote(part(other), body.at[core, span(other)], (0, 0), (gx, gy, other)))
    for send in sends:
        send.start()

    body[core, span(core)] = packed[pl.ds(3 * core, SENT)]
    for load in loads[4:]:
        load.wait()

    y_first = gy * BY + core * HY - 2
    row = iota((YY * SUB, 64), 0)
    sub = row & (SUB - 1)
    row_x = gx * BX + jnp.where(sub < 12, sub, sub - SUB)
    row_y = y_first + (row >> 4)
    hit = (row_x == cells_v[0:1, :]) & (row_y == cells_v[1:2, :])
    hit_z = jnp.where(iota((LANES, 64), 0) == cells_v[2:3, :], 1.0, 0.0)
    for c in range(3):
        left = jnp.where(hit, amps_v[c : c + 1, :], 0.0)
        source[c] = lax.dot_general(
            left, hit_z, (((1,), (1,)), ((), ())),
            precision=lax.Precision.HIGHEST, preferred_element_type=jnp.float32,
        ).reshape(YY, SUB, LANES)

    shape = (BX, LANES)
    r = iota(shape, 0)
    omega = jnp.zeros(shape, jnp.float32)
    for f in range(FREQ):
        omega = jnp.where((r & 3) == f, omegas[f], omega)
    phase = omega * ((r >> 2) + 1).astype(jnp.float32)
    cosine = jnp.cos(phase)
    sine = -jnp.sin(phase)
    square = omega * omega

    for t in (0, 1):
        lanes = pl.ds(LANES * t, LANES)
        design = 0.05 * mask_v[:, lanes].astype(jnp.float32)
        for c in range(3):
            gains = [jnp.zeros((BX, LANES), jnp.float32)] * 2
            for f in range(FREQ):
                real = square[f : f + 1, :] * fwd_v[t, pl.ds(3 * f + c, BX, stride=6 * FREQ), :]
                imag = square[f : f + 1, :] * fwd_v[t, pl.ds(3 * FREQ + 3 * f + c, BX, stride=6 * FREQ), :]
                for n in (0, 1):
                    k = FREQ * n + f
                    gains[n] = gains[n] + cosine[k : k + 1, :] * real - sine[k : k + 1, :] * imag
            for n in (0, 1):
                gain[n, c, :, lanes] = design * gains[n]

    remote(part(core), body.at[other, span(core)], (0, 0), (gx, gy, other)).wait_recv()
    for h in (0, 1):
        remote(packed.at[0], body.at[h, 5 * core], (0, 1 + h), (gx, gy, other)).wait_recv()
        for side in (0, 1):
            place = pl.ds(48 * side, 16)
            remote(edge.at[0, pl.ds(0, SENT)], halo.at[h, span(core), place], (0, 3 + 2 * side + h), (gx, gy, other)).wait_recv()
            remote(edge.at[0, 0], halo.at[h, 5 * core, place], (0, 7 + 2 * side + h), (gx, gy, other)).wait_recv()

    x_of = iota((SUB, LANES), 0)
    x_of = gx * BX + jnp.where(x_of < 12, x_of, x_of - SUB)
    lane = iota((SUB, LANES), 1)
    inside = (x_of >= 0) & (x_of < nx * BX) & (lane < DEPTH)
    y_end = ny * BY

    lane_b = iota((ROWS, LANES), 1)
    lane_h = iota((64, LANES), 1)

    def merge(low, high, lanes):
        even = jnp.where(lanes < CZ, low, roll(high, CZ, 1))
        odd = jnp.where(lanes < CZ, roll(low, -CZ, 1), high)
        return even, odd

    for pair in range(YY // 2):
        own = merge(body[0, pair], body[1, pair], lane_b)
        beside = merge(halo[0, pair], halo[1, pair], lane_h)
        for k in (0, 1):
            merged[k] = beside[k]
            yy = 2 * pair + k
            y = y_first + yy
            ok = inside & (y >= 0) & (y < y_end)
            for j in range(COMPS):
                tile = jnp.concatenate([own[k][BX * j : BX * j + BX], merged[k, pl.ds(j, 8, stride=8), :]], axis=0)
                fields[j, yy] = jnp.where(ok, tile, 0.0)

    half = jnp.where(inside, COURANT, 0.0)

    def magnetic_rows(first, last):
        def step(yy, carry):
            e0, e1, e2 = fields[0, yy], fields[1, yy], fields[2, yy]
            n0, n2 = fields[0, yy + 1], fields[2, yy + 1]
            y = y_first + yy
            scale = jnp.where((y >= 0) & (y < y_end), half, 0.0)
            fields[3, yy] = fields[3, yy] - scale * ((n2 - e2) - (roll(e1, -1, 1) - e1))
            fields[4, yy] = fields[4, yy] - scale * ((roll(e0, -1, 1) - e0) - (roll(e2, -1, 0) - e2))
            fields[5, yy] = fields[5, yy] - scale * ((roll(e1, -1, 0) - e1) - (n0 - e0))
            return carry

        lax.fori_loop(first, last, step, 0, unroll=True)

    def electric_rows(first, last, time):
        factor = math.cos(0.7 * (time + 0.5))

        def step(yy, carry):
            h0, h1, h2 = fields[3, yy], fields[4, yy], fields[5, yy]
            p0, p2 = fields[3, yy - 1], fields[5, yy - 1]
            scale = fields[6, yy]
            curls = (
                (h2 - p2) - (h1 - roll(h1, 1, 1)),
                (h0 - roll(h0, 1, 1)) - (h2 - roll(h2, 1, 0)),
                (h1 - roll(h1, 1, 0)) - (h0 - p0),
            )
            for c in range(3):
                fields[c, yy] = fields[c, yy] + scale * (curls[c] - factor * source[c, yy])
            return carry

        lax.fori_loop(first, last, step, 0, unroll=True)

    quarter = iota((BX, LANES), 1) >> 5

    def flatten(time):
        for c in range(3):
            for tile in (0, 1):
                out = jnp.zeros((BX, LANES), jnp.float32)
                for q in range(4):
                    v = fields[c, 2 + 4 * tile + q, 0:BX, :]
                    out = jnp.where(quarter == q, roll(v, SLAB * q - BOTTOM, 1), out)
                flat[time, c, :, pl.ds(LANES * tile, LANES)] = out

    magnetic_rows(0, 11)
    electric_rows(1, 11, 0)
    flatten(0)
    magnetic_rows(1, 10)
    electric_rows(2, 10, 1)
    flatten(1)

    shape = (BX, 2 * LANES)
    total = jnp.zeros(shape, jnp.float32)
    for n in (0, 1):
        for c in range(3):
            total = total + gain[n, c] * flat[n, c]

    z = iota(shape, 1) & (SLAB - 1)
    folded = total
    for by in (-2, -1, 1, 2):
        ok = same_pixel(z, anchor[2], by) & (z + by >= 0) & (z + by < SLAB)
        folded = folded + jnp.where(ok, roll(total, -by, 1), 0.0)
    g_send[...] = folded

    above = (gx, jnp.where(core == 0, gy, up_y), other)
    below = (gx, jnp.where(core == 0, down_y, gy), other)
    first_rows, last_rows = g_send.at[:, pl.ds(0, LANES)], g_send.at[:, pl.ds(LANES, LANES)]
    swaps = [
        remote(first_rows, g_y.at[0], (12, 12), below),
        remote(last_rows, g_y.at[1], (13, 13), above),
        remote(first_rows, g_c.at[0, 0], (14, 14), (down_x,) + below[1:]),
        remote(last_rows, g_c.at[0, 1], (15, 15), (down_x,) + above[1:]),
        remote(first_rows, g_c.at[1, 0], (16, 16), (up_x,) + below[1:]),
        remote(last_rows, g_c.at[1, 1], (17, 17), (up_x,) + above[1:]),
        remote(g_send, g_x.at[0], (18, 18), (down_x, gy, core)),
        remote(g_send, g_x.at[1], (19, 19), (up_x, gy, core)),
    ]
    for swap in swaps:
        swap.start()

    for y in range(HY):
        v = jnp.concatenate([fields[c, 2 + y, 0:BX, :] for c in range(3)], axis=0)
        moved = roll(v, -CZ, 1)
        first = core == 0
        fe[pl.ds(HY * core + y, 3 * BX, stride=BY), :] = jnp.where(first, v, moved)[:, :CZ]
        fe_send[y] = jnp.where(first, moved, v)
    fe_copy = remote(fe_send, fe_recv, (11, 11), (gx, gy, other))
    fe_copy.start()

    for t in (0, 1):
        lanes = pl.ds(LANES * t, LANES)
        for f in range(FREQ):
            for p, weights in ((0, cosine), (1, sine)):
                for c in range(3):
                    rows = pl.ds(3 * FREQ * p + 3 * f + c, BX, stride=6 * FREQ)
                    adj_v[t, rows, :] = (
                        weights[f : f + 1, :] * flat[0, c, :, lanes]
                        + weights[FREQ + f : FREQ + f + 1, :] * flat[1, c, :, lanes]
                    )
    stores = [
        pltpu.make_async_copy(adj_v.at[t], adj.at[:, pl.ds(LANES * t, LANES)], load_sem.at[11 + t]) for t in (0, 1)
    ]
    for store in stores:
        store.start()

    fe_copy.wait_recv()
    for y in range(HY):
        fe[pl.ds(HY * other + y, 3 * BX, stride=BY), :] = fe_recv[y][:, :CZ]

    for swap in swaps:
        swap.wait_recv()
    block = gy * 2 + core
    wide = (BX, 4 * LANES)
    tile0 = jnp.concatenate([folded, g_y[0], g_y[1]], axis=1)
    upper = jnp.concatenate([g_x[0], g_c[0, 0], g_c[0, 1]], axis=1)
    lower = jnp.concatenate([g_x[1], g_c[1, 0], g_c[1, 1]], axis=1)
    x_row, column = iota(wide, 0), iota(wide, 1)
    upper = jnp.where(gx < nx - 1, upper, 0.0)
    lower = jnp.where(gx > 0, lower, 0.0)
    tile1 = jnp.where(x_row < 4, upper, lower)
    y_ok = (column < 2 * LANES) | ((column < 3 * LANES) & (block < 2 * ny - 1)) | ((column >= 3 * LANES) & (block > 0))
    extended = jnp.where(
        jnp.concatenate([y_ok, y_ok], axis=0), jnp.concatenate([tile0, tile1], axis=0), 0.0
    )
    along_x = extended[:BX]
    for by in (-2, -1, 1, 2):
        ok = same_pixel(gx * BX + x_row, anchor[0], by)
        along_x = along_x + jnp.where(ok, roll(extended, -by, 0)[:BX], 0.0)
    result = along_x[:, : 2 * LANES]
    y_row = block * HY + (iota(shape, 1) >> 5)
    for by in (-2, -1, 1, 2):
        ok = same_pixel(y_row, anchor[1], by)
        result = result + jnp.where(ok, roll(along_x, -SLAB * by, 1)[:, : 2 * LANES], 0.0)
    grad[...] = result

    for send in sends + [fe_copy] + swaps:
        send.wait_send()
    for store in stores:
        store.wait()


def deliver(adj, grad, fe, adj_out, grad_out, fe_out, sem):
    copies = [
        pltpu.make_async_copy(src, dst, sem.at[i])
        for i, (src, dst) in enumerate([(adj, adj_out), (fe, fe_out), (grad, grad_out)])
    ]
    for copy in copies:
        copy.start()
    for copy in copies:
        copy.wait()


def body_fn(
    electric, magnetic, material, permittivity, source_cells, amplitudes, omegas, design_mask, forward_dft, pixel_anchor
):
    f32 = jnp.float32
    anywhere = pl.BlockSpec(memory_space=pl.ANY)
    vmem = pl.BlockSpec(memory_space=pltpu.VMEM)
    adj, grad, fe = pl.pallas_call(
        kernel,
        out_shape=(
            jax.ShapeDtypeStruct((BX * 6 * FREQ, 2 * LANES), f32),
            jax.ShapeDtypeStruct((BX, 2 * LANES), f32),
            jax.ShapeDtypeStruct((3 * BX * BY, CZ), f32),
        ),
        in_specs=[anywhere] * 10,
        out_specs=(anywhere, vmem, vmem),
        scratch_shapes=[
            pltpu.SMEM((MATS,), f32),
            pltpu.SMEM((FREQ,), f32),
            pltpu.SMEM((3,), jnp.int32),
            pltpu.VMEM((3 * BX * BY, CZ), f32),
            pltpu.VMEM((3 * BX * BY, CZ), f32),
            pltpu.VMEM((BX * BY, CZ), jnp.int32),
            pltpu.VMEM((3, 64), jnp.int32),
            pltpu.VMEM((3, 64), f32),
            pltpu.VMEM((BX, 2 * LANES), jnp.int32),
            pltpu.VMEM((2, BX * 6 * FREQ, LANES), f32),
            pltpu.VMEM((2, BX * 6 * FREQ, LANES), f32),
            pltpu.VMEM((BX * BY, CZ), f32),
            pltpu.VMEM((PAIRS, ROWS, LANES), f32),
            pltpu.VMEM((2, PAIRS, 16, LANES), f32),
            pltpu.VMEM((2, YY // 2, ROWS, LANES), f32),
            pltpu.VMEM((2, YY // 2, 64, LANES), f32),
            pltpu.VMEM((2, 64, LANES), f32),
            pltpu.VMEM((COMPS, YY, SUB, LANES), f32),
            pltpu.VMEM((3, YY, SUB, LANES), f32),
            pltpu.VMEM((2, 3, BX, 2 * LANES), f32),
            pltpu.VMEM((2, 3, BX, 2 * LANES), f32),
            pltpu.VMEM((HY, 3 * BX, LANES), f32),
            pltpu.VMEM((HY, 3 * BX, LANES), f32),
            pltpu.VMEM((BX, 2 * LANES), f32),
            pltpu.VMEM((2, BX, 2 * LANES), f32),
            pltpu.VMEM((2, BX, LANES), f32),
            pltpu.VMEM((2, 2, BX, LANES), f32),
            pltpu.SemaphoreType.DMA((13,)),
            pltpu.SemaphoreType.DMA((20,)),
            pltpu.SemaphoreType.DMA((20,)),
        ],
        compiler_params=pltpu.CompilerParams(
            collective_id=0, has_side_effects=True, vmem_limit_bytes=24 * 1024 * 1024
        ),
    )(
        *[
            pltpu.with_memory_space_constraint(v, pltpu.HBM)
            for v in (
                electric.reshape(3 * BX * BY, CZ),
                magnetic.reshape(3 * BX * BY, CZ),
                material.reshape(BX * BY, CZ),
                permittivity,
                source_cells.T,
                amplitudes.T,
                omegas,
                design_mask,
                forward_dft.reshape(BX * 6 * FREQ, 2 * LANES),
                pixel_anchor,
            )
        ]
    )
    adj, grad, fe = pl.pallas_call(
        deliver,
        out_shape=tuple(jax.ShapeDtypeStruct(v.shape, f32) for v in (adj, grad, fe)),
        in_specs=[anywhere] * 3,
        out_specs=(anywhere,) * 3,
        scratch_shapes=[pltpu.SemaphoreType.DMA((3,))],
        compiler_params=pltpu.CompilerParams(vmem_limit_bytes=1024 * 1024),
    )(adj, grad, fe)
    return adj.reshape(BX, 6 * FREQ, 2 * LANES), grad, fe.reshape(3, BX, BY, CZ)


def solution(mesh):
    return jax.shard_map(
        body_fn,
        mesh=mesh,
        in_specs=(
            P(None, "gx", "gy", "gz"),
            P(None, "gx", "gy", "gz"),
            P("gx", "gy", "gz"),
            P(),
            P(),
            P(),
            P(),
            P("gx", ("gy", "gz")),
            P("gx", None, ("gy", "gz")),
            P(),
        ),
        out_specs=(P("gx", None, ("gy", "gz")), P("gx", ("gy", "gz")), P(None, "gx", "gy", "gz")),
        check_vma=False,
    )
```

```python
import math

import jax
import jax.numpy as jnp
from jax import lax
from jax.experimental import pallas as pl
from jax.experimental.pallas import tpu as pltpu
from jax.sharding import PartitionSpec as P

SLAB = 32
FREQ = 4
MATS = 4
COURANT = 0.5

BX, BY, CZ = 8, 16, 48
HY = BY // 2
LANES = 128
DEPTH = 2 * CZ
BOTTOM = CZ // 4
COMPS = 7
ROWS = COMPS * BX
PAIRS = BY // 2
WIDE = 4
YY = HY + 2 * WIDE
SUB = BX + 2 * WIDE


def roll(v, by, axis):
    return pltpu.roll(v, by % v.shape[axis], axis)


def iota(shape, axis):
    return lax.broadcasted_iota(jnp.int32, shape, axis)


def third(v):
    return (v * 21846) >> 16


def same_pixel(coord, anchor, by):
    shifted = coord + anchor
    place = shifted - 3 * third(shifted) + by
    return (place >= 0) & (place <= 2)


def kernel(
    e_in, h_in, mat_in, perm_in, cells_in, amps_in, omegas_in, mask_in, fwd_in, anchor_in,
    adj, grad, fe,
    perm, omegas, anchor,
    e_v, h_v, mat_v, cells_v, amps_v, mask_v, fwd_v, adj_v, coef_v,
    packed, edge, body0, body1, halo0, halo1, merged, fields, source, gain, flat,
    fe_send, fe_recv, sx, sy, sc, g_x, g_y, g_c,
    load_sem, send_sem, recv_sem,
):
    nx, ny = lax.axis_size("gx"), lax.axis_size("gy")
    gx, gy, core = lax.axis_index("gx"), lax.axis_index("gy"), lax.axis_index("gz")
    other = 1 - core
    up_x, down_x = lax.rem(gx + 1, nx), lax.rem(gx + nx - 1, nx)
    up_y, down_y = lax.rem(gy + 1, ny), lax.rem(gy + ny - 1, ny)

    barrier = pltpu.get_barrier_semaphore()
    face_y = jnp.where(core == 0, down_y, up_y)
    senders = [(gx, gy, other)]
    for h in (0, 1):
        senders += [(up_x, gy, h), (down_x, gy, h)]
        senders += [(gx, face_y, h), (up_x, face_y, h), (down_x, face_y, h)]
    for sender in senders:
        pl.semaphore_signal(barrier, inc=1, device_id=sender, device_id_type=pl.DeviceIdType.MESH)

    loads = [
        pltpu.make_async_copy(src, dst, load_sem.at[i])
        for i, (src, dst) in enumerate(
            [(perm_in, perm), (mat_in, mat_v), (e_in, e_v), (h_in, h_v), (cells_in, cells_v), (amps_in, amps_v),
             (omegas_in, omegas), (anchor_in, anchor), (mask_in, mask_v)]
            + [(fwd_in.at[:, pl.ds(LANES * t, LANES)], fwd_v.at[t]) for t in (0, 1)]
        )
    ]
    for load in loads:
        load.start()

    edge[...] = jnp.zeros_like(edge)
    halo1[:, 16:48, :] = jnp.zeros((PAIRS - 2, 32, LANES), jnp.float32)

    for load in loads[:4]:
        load.wait()
    material = mat_v[...]
    eps = jnp.zeros(material.shape, jnp.float32)
    for level in range(MATS):
        eps = eps + jnp.where(material == level, perm[level], 0.0)
    coef_v[...] = COURANT / eps
    blank = jnp.zeros((ROWS, LANES - DEPTH), jnp.float32)
    for pair in range(PAIRS):
        rows = [
            jnp.concatenate(
                [
                    e_v[pl.ds(y, 3 * BX, stride=BY), :],
                    h_v[pl.ds(y, 3 * BX, stride=BY), :],
                    coef_v[pl.ds(y, BX, stride=BY), :],
                ],
                axis=0,
            )
            for y in (2 * pair, 2 * pair + 1)
        ]
        packed[pair] = jnp.concatenate(rows + [blank], axis=1)
    for pair in range(PAIRS):
        for side in (0, 1):
            for x in range(WIDE):
                edge[side, pair, pl.ds(8 * x, COMPS), :] = packed[pair, pl.ds(WIDE * side + x, COMPS, stride=BX), :]
    for load in loads[4:]:
        load.wait()

    shape = (BX, LANES)
    r = iota(shape, 0)
    omega = jnp.zeros(shape, jnp.float32)
    for f in range(FREQ):
        omega = jnp.where((r & 3) == f, omegas[f], omega)
    phase = omega * ((r >> 2) + 1).astype(jnp.float32)
    cosine = jnp.cos(phase)
    sine = -jnp.sin(phase)
    square = omega * omega

    for t in (0, 1):
        lanes = pl.ds(LANES * t, LANES)
        design = 0.05 * mask_v[:, lanes].astype(jnp.float32)
        for c in range(3):
            gains = [jnp.zeros((BX, LANES), jnp.float32)] * 2
            for f in range(FREQ):
                real = square[f : f + 1, :] * fwd_v[t, pl.ds(3 * f + c, BX, stride=6 * FREQ), :]
                imag = square[f : f + 1, :] * fwd_v[t, pl.ds(3 * FREQ + 3 * f + c, BX, stride=6 * FREQ), :]
                for n in (0, 1):
                    k = FREQ * n + f
                    gains[n] = gains[n] + cosine[k : k + 1, :] * real - sine[k : k + 1, :] * imag
            for n in (0, 1):
                gain[n, c, :, lanes] = design * gains[n]

    lane_g = iota((BX, LANES), 1)
    firsts, lasts = [], []
    for n, c in ((0, 0), (0, 2), (1, 1)):
        one, two = gain[n, c], gain[n + (c == 2), (c + 1) % 3]
        firsts.append(jnp.where(lane_g < 64, one[:, :LANES], roll(two[:, :LANES], 64, 1)))
        lasts.append(jnp.where(lane_g < 64, roll(two[:, LANES:], 64, 1), one[:, LANES:]))
    none2, none4 = jnp.zeros((2, LANES), jnp.float32), jnp.zeros((4, 2 * LANES), jnp.float32)
    for side, x in ((0, 0), (1, BX - 2)):
        sx[side] = jnp.concatenate([gain[n, c, x : x + 2, :] for n in (0, 1) for c in range(3)] + [none4], axis=0)
        for k, tiles in ((0, firsts), (1, lasts)):
            sc[side, k] = jnp.concatenate([t[x : x + 2] for t in tiles] + [none2], axis=0)
    for m in range(3):
        sy[0, m], sy[1, m] = firsts[m], lasts[m]

    def remote(src, dst, role, device):
        return pltpu.make_async_remote_copy(
            src_ref=src,
            dst_ref=dst,
            send_sem=send_sem.at[role[0]],
            recv_sem=recv_sem.at[role[1]],
            device_id=device,
            device_id_type=pl.DeviceIdType.MESH,
        )

    def sends_of(half):
        if half == 0:
            last, first, low, high = pl.ds(6, 2), pl.ds(0, 2), pl.ds(0, 6), pl.ds(2, 6)
            body, halo, at_low, at_high = body0, halo0, pl.ds(0, 2), pl.ds(6, 2)
            to_low, to_high = pl.ds(2, 6), pl.ds(0, 6)
            rows, places = (pl.ds(0, 32), pl.ds(0, 32)), (pl.ds(0, 32), pl.ds(32, 32))
        else:
            last, first, low, high = pl.ds(7, 1), pl.ds(0, 1), pl.ds(0, 5), pl.ds(3, 5)
            body, halo, at_low, at_high = body1, halo1, pl.ds(0, 1), pl.ds(5, 1)
            to_low, to_high = pl.ds(1, 5), pl.ds(0, 5)
            rows, places = (pl.ds(0, 16), pl.ds(16, 16)), (pl.ds(0, 16), pl.ds(48, 16))
        sides = ((0, down_x), (1, up_x))
        sends = []
        for side, to_x in sides:
            row, place = rows[side], places[side]
            role = 7 + 2 * side + half
            sends += [
                remote(edge.at[side, last, row], halo.at[at_low, place], (3 + 4 * side, role), (to_x, up_y, 0)),
                remote(edge.at[side, first, row], halo.at[at_high, place], (4 + 4 * side, role), (to_x, down_y, 1)),
            ]
        sends += [
            remote(packed.at[last], body.at[at_low], (1, 1 + half), (gx, up_y, 0)),
            remote(packed.at[first], body.at[at_high], (2, 1 + half), (gx, down_y, 1)),
        ]
        for side, to_x in sides:
            row, place = rows[side], places[side]
            role = 3 + 2 * side + half
            sends += [
                remote(edge.at[side, low, row], halo.at[to_low, place], (5 + 4 * side, role), (to_x, gy, 0)),
                remote(edge.at[side, high, row], halo.at[to_high, place], (6 + 4 * side, role), (to_x, gy, 1)),
            ]
        part, span = (high, to_high) if half == 0 else (low, to_low)
        sends.append(remote(packed.at[part], body.at[span], (0, 0), (gx, gy, 1 - half)))
        return sends

    above = (gx, jnp.where(core == 0, gy, up_y), other)
    below = (gx, jnp.where(core == 0, down_y, gy), other)
    swaps = [
        remote(sc.at[0, 0], g_c.at[0, 0], (14, 14), (down_x,) + below[1:]),
        remote(sc.at[0, 1], g_c.at[0, 1], (15, 15), (down_x,) + above[1:]),
        remote(sc.at[1, 0], g_c.at[1, 0], (16, 16), (up_x,) + below[1:]),
        remote(sc.at[1, 1], g_c.at[1, 1], (17, 17), (up_x,) + above[1:]),
        remote(sy.at[0], g_y.at[0], (12, 12), below),
        remote(sy.at[1], g_y.at[1], (13, 13), above),
        remote(sx.at[0], g_x.at[0], (18, 18), (down_x, gy, core)),
        remote(sx.at[1], g_x.at[1], (19, 19), (up_x, gy, core)),
    ]

    pl.semaphore_wait(barrier, len(senders))
    for half in (0, 1):
        @pl.when(core == half)
        def _(half=half):
            for send in sends_of(half):
                send.start()
            if half == 0:
                body0[2:8] = packed[0:6]
            else:
                body1[0:5] = packed[3:8]
    for swap in swaps:
        swap.start()

    y_first = gy * BY + core * HY - WIDE
    row = iota((YY * SUB, 64), 0)
    sub = row & (SUB - 1)
    row_x = gx * BX + jnp.where(sub < 12, sub, sub - SUB)
    row_y = y_first + (row >> 4)
    hit = (row_x == cells_v[0:1, :]) & (row_y == cells_v[1:2, :])
    hit_z = jnp.where(iota((LANES, 64), 0) == cells_v[2:3, :], 1.0, 0.0)
    for c in range(3):
        left = jnp.where(hit, amps_v[c : c + 1, :], 0.0)
        source[c] = lax.dot_general(
            left, hit_z, (((1,), (1,)), ((), ())),
            precision=lax.Precision.HIGHEST, preferred_element_type=jnp.float32,
        ).reshape(YY, SUB, LANES)

    here = (gx, gy, other)
    for half in (0, 1):
        @pl.when(core != half)
        def _(half=half):
            if half == 0:
                remote(packed.at[pl.ds(2, 6)], body0.at[pl.ds(0, 6)], (0, 0), here).wait_recv()
            else:
                remote(packed.at[pl.ds(0, 5)], body1.at[pl.ds(1, 5)], (0, 0), here).wait_recv()

        body, halo = (body0, halo0) if half == 0 else (body1, halo1)
        face, long, rows = (2, 6, 32) if half == 0 else (1, 5, 16)
        at_face = pl.ds(6 * core if half == 0 else 5 * core, face)
        span = pl.ds(2 - 2 * core if half == 0 else 1 - core, long)
        remote(packed.at[pl.ds(0, face)], body.at[at_face], (0, 1 + half), here).wait_recv()
        for side in (0, 1):
            place = pl.ds((64 - rows) * side, rows)
            x_part, corner = edge.at[0, pl.ds(0, long), pl.ds(0, rows)], edge.at[0, pl.ds(0, face), pl.ds(0, rows)]
            remote(x_part, halo.at[span, place], (0, 3 + 2 * side + half), here).wait_recv()
            remote(corner, halo.at[at_face, place], (0, 7 + 2 * side + half), here).wait_recv()

    x_of = iota((SUB, LANES), 0)
    x_of = gx * BX + jnp.where(x_of < 12, x_of, x_of - SUB)
    lane = iota((SUB, LANES), 1)
    inside = (x_of >= 0) & (x_of < nx * BX) & (lane < DEPTH)
    y_end = ny * BY

    lane_b = iota((ROWS, LANES), 1)
    lane_h = iota((64, LANES), 1)

    def merge(low, high, lanes):
        even = jnp.where(lanes < CZ, low, roll(high, CZ, 1))
        odd = jnp.where(lanes < CZ, roll(low, -CZ, 1), high)
        return even, odd

    for pair in range(YY // 2):
        if 1 <= pair <= PAIRS - 2:
            upper_own, upper_beside = body1[pair - 1], halo1[pair - 1]
        else:
            upper_own, upper_beside = jnp.zeros((ROWS, LANES), jnp.float32), jnp.zeros((64, LANES), jnp.float32)
        own = merge(body0[pair], upper_own, lane_b)
        beside = merge(halo0[pair], upper_beside, lane_h)
        for k in (0, 1):
            merged[k] = beside[k]
            yy = 2 * pair + k
            y = y_first + yy
            ok = inside & (y >= 0) & (y < y_end)
            for j in range(COMPS):
                tile = jnp.concatenate([own[k][BX * j : BX * j + BX], merged[k, pl.ds(j, 8, stride=8), :]], axis=0)
                fields[j, yy] = jnp.where(ok, tile, 0.0)

    half = jnp.where(inside, COURANT, 0.0)

    def magnetic_rows(first, last):
        def step(yy, carry):
            e0, e1, e2 = fields[0, yy], fields[1, yy], fields[2, yy]
            n0, n2 = fields[0, yy + 1], fields[2, yy + 1]
            y = y_first + yy
            scale = jnp.where((y >= 0) & (y < y_end), half, 0.0)
            fields[3, yy] = fields[3, yy] - scale * ((n2 - e2) - (roll(e1, -1, 1) - e1))
            fields[4, yy] = fields[4, yy] - scale * ((roll(e0, -1, 1) - e0) - (roll(e2, -1, 0) - e2))
            fields[5, yy] = fields[5, yy] - scale * ((roll(e1, -1, 0) - e1) - (n0 - e0))
            return carry

        lax.fori_loop(first, last, step, 0, unroll=True)

    def electric_rows(first, last, time):
        factor = math.cos(0.7 * (time + 0.5))

        def step(yy, carry):
            h0, h1, h2 = fields[3, yy], fields[4, yy], fields[5, yy]
            p0, p2 = fields[3, yy - 1], fields[5, yy - 1]
            scale = fields[6, yy]
            curls = (
                (h2 - p2) - (h1 - roll(h1, 1, 1)),
                (h0 - roll(h0, 1, 1)) - (h2 - roll(h2, 1, 0)),
                (h1 - roll(h1, 1, 0)) - (h0 - p0),
            )
            for c in range(3):
                fields[c, yy] = fields[c, yy] + scale * (curls[c] - factor * source[c, yy])
            return carry

        lax.fori_loop(first, last, step, 0, unroll=True)

    quarter = iota((SUB, LANES), 1) >> 5

    def flatten(time):
        for c in range(3):
            for tile, first, quarters in ((0, 0, range(4)), (1, 4, range(4)), (2, 8, (0, 1)), (3, -4, (2, 3))):
                out = jnp.zeros((SUB, LANES), jnp.float32)
                for q in quarters:
                    v = fields[c, WIDE + first + q]
                    out = jnp.where(quarter == q, roll(v, SLAB * q - BOTTOM, 1), out)
                flat[time, c, :, pl.ds(LANES * tile, LANES)] = out

    magnetic_rows(0, YY - 1)
    electric_rows(1, YY - 1, 0)
    flatten(0)
    magnetic_rows(1, YY - 2)
    electric_rows(2, YY - 2, 1)

    for y in range(HY):
        v = jnp.concatenate([fields[c, WIDE + y, 0:BX, :] for c in range(3)], axis=0)
        moved = roll(v, -CZ, 1)
        first = core == 0
        fe[pl.ds(HY * core + y, 3 * BX, stride=BY), :] = jnp.where(first, v, moved)[:, :CZ]
        fe_send[y] = jnp.where(first, moved, v)
    fe_copy = remote(fe_send, fe_recv, (11, 11), (gx, gy, other))
    fe_copy.start()

    flatten(1)

    for t in (0, 1):
        lanes = pl.ds(LANES * t, LANES)
        for f in range(FREQ):
            for p, weights in ((0, cosine), (1, sine)):
                for c in range(3):
                    rows = pl.ds(3 * FREQ * p + 3 * f + c, BX, stride=6 * FREQ)
                    adj_v[t, rows, :] = (
                        weights[f : f + 1, :] * flat[0, c, 0:BX, lanes]
                        + weights[FREQ + f : FREQ + f + 1, :] * flat[1, c, 0:BX, lanes]
                    )
    stores = [
        pltpu.make_async_copy(adj_v.at[t], adj.at[:, pl.ds(LANES * t, LANES)], load_sem.at[11 + t]) for t in (0, 1)
    ]
    for store in stores:
        store.start()

    for swap in swaps:
        swap.wait_recv()
    block = gy * 2 + core
    wide = (SUB, 4 * LANES)
    total = jnp.zeros(wide, jnp.float32)
    gap2 = jnp.zeros((4, 2 * LANES), jnp.float32)
    gap1 = jnp.zeros((4, LANES), jnp.float32)
    for n in (0, 1):
        for c in range(3):
            k = 3 * n + c
            two = pl.ds(2 * k, 2)
            pair = pl.ds(2 * (k // 2), 2)
            tile1 = jnp.concatenate([g_x[0, two, :], gap2, g_x[1, two, :]], axis=0)
            beyond = []
            for up in (0, 1):
                corner = jnp.concatenate([g_c[0, up, pair, :], gap1, g_c[1, up, pair, :]], axis=0)
                both = jnp.concatenate([g_y[up, k // 2], corner], axis=0)
                beyond.append(roll(both, 64, 1) if k % 2 else both)
            weight = jnp.concatenate([jnp.concatenate([gain[n, c], tile1], axis=0)] + beyond, axis=1)
            total = total + weight * flat[n, c]
    row, column = iota(wide, 0), iota(wide, 1)
    x_all = gx * BX + jnp.where(row < 12, row, row - SUB)
    here_ok = (x_all >= 0) & (x_all < nx * BX)
    here_ok = here_ok & ((column < 3 * LANES) | (block > 0)) & ((column < 2 * LANES) | (column >= 3 * LANES) | (block < 2 * ny - 1))
    total = jnp.where(here_ok, total, 0.0)

    z = column & (SLAB - 1)
    extended = total
    for by in (-2, -1, 1, 2):
        ok = same_pixel(z, anchor[2], by) & (z + by >= 0) & (z + by < SLAB)
        extended = extended + jnp.where(ok, roll(total, -by, 1), 0.0)
    x_row = gx * BX + iota((BX, 4 * LANES), 0)
    along_x = extended[:BX]
    for by in (-2, -1, 1, 2):
        ok = same_pixel(x_row, anchor[0], by)
        along_x = along_x + jnp.where(ok, roll(extended, -by, 0)[:BX], 0.0)
    shape = (BX, 2 * LANES)
    result = along_x[:, : 2 * LANES]
    y_row = block * HY + (iota(shape, 1) >> 5)
    for by in (-2, -1, 1, 2):
        ok = same_pixel(y_row, anchor[1], by)
        result = result + jnp.where(ok, roll(along_x, -SLAB * by, 1)[:, : 2 * LANES], 0.0)
    grad[...] = result

    fe_copy.wait_recv()
    for y in range(HY):
        fe[pl.ds(HY * other + y, 3 * BX, stride=BY), :] = fe_recv[y][:, :CZ]

    for half in (0, 1):
        @pl.when(core == half)
        def _(half=half):
            for send in sends_of(half):
                send.wait_send()
    for send in [fe_copy] + swaps:
        send.wait_send()
    for store in stores:
        store.wait()


def deliver(adj, grad, fe, adj_out, grad_out, fe_out, sem):
    copies = [
        pltpu.make_async_copy(src, dst, sem.at[i])
        for i, (src, dst) in enumerate([(adj, adj_out), (fe, fe_out), (grad, grad_out)])
    ]
    for copy in copies:
        copy.start()
    for copy in copies:
        copy.wait()


def body_fn(
    electric, magnetic, material, permittivity, source_cells, amplitudes, omegas, design_mask, forward_dft, pixel_anchor
):
    f32 = jnp.float32
    anywhere = pl.BlockSpec(memory_space=pl.ANY)
    vmem = pl.BlockSpec(memory_space=pltpu.VMEM)
    adj, grad, fe = pl.pallas_call(
        kernel,
        out_shape=(
            jax.ShapeDtypeStruct((BX * 6 * FREQ, 2 * LANES), f32),
            jax.ShapeDtypeStruct((BX, 2 * LANES), f32),
            jax.ShapeDtypeStruct((3 * BX * BY, CZ), f32),
        ),
        in_specs=[anywhere] * 10,
        out_specs=(anywhere, vmem, vmem),
        scratch_shapes=[
            pltpu.SMEM((MATS,), f32),
            pltpu.SMEM((FREQ,), f32),
            pltpu.SMEM((3,), jnp.int32),
            pltpu.VMEM((3 * BX * BY, CZ), f32),
            pltpu.VMEM((3 * BX * BY, CZ), f32),
            pltpu.VMEM((BX * BY, CZ), jnp.int32),
            pltpu.VMEM((3, 64), jnp.int32),
            pltpu.VMEM((3, 64), f32),
            pltpu.VMEM((BX, 2 * LANES), jnp.int32),
            pltpu.VMEM((2, BX * 6 * FREQ, LANES), f32),
            pltpu.VMEM((2, BX * 6 * FREQ, LANES), f32),
            pltpu.VMEM((BX * BY, CZ), f32),
            pltpu.VMEM((PAIRS, ROWS, LANES), f32),
            pltpu.VMEM((2, PAIRS, 8 * WIDE, LANES), f32),
            pltpu.VMEM((PAIRS, ROWS, LANES), f32),
            pltpu.VMEM((PAIRS - 2, ROWS, LANES), f32),
            pltpu.VMEM((PAIRS, 64, LANES), f32),
            pltpu.VMEM((PAIRS - 2, 64, LANES), f32),
            pltpu.VMEM((2, 64, LANES), f32),
            pltpu.VMEM((COMPS, YY, SUB, LANES), f32),
            pltpu.VMEM((3, YY, SUB, LANES), f32),
            pltpu.VMEM((2, 3, BX, 2 * LANES), f32),
            pltpu.VMEM((2, 3, SUB, 4 * LANES), f32),
            pltpu.VMEM((HY, 3 * BX, LANES), f32),
            pltpu.VMEM((HY, 3 * BX, LANES), f32),
            pltpu.VMEM((2, 16, 2 * LANES), f32),
            pltpu.VMEM((2, 3, BX, LANES), f32),
            pltpu.VMEM((2, 2, BX, LANES), f32),
            pltpu.VMEM((2, 16, 2 * LANES), f32),
            pltpu.VMEM((2, 3, BX, LANES), f32),
            pltpu.VMEM((2, 2, BX, LANES), f32),
            pltpu.SemaphoreType.DMA((13,)),
            pltpu.SemaphoreType.DMA((20,)),
            pltpu.SemaphoreType.DMA((20,)),
        ],
        compiler_params=pltpu.CompilerParams(
            collective_id=0, has_side_effects=True, vmem_limit_bytes=24 * 1024 * 1024
        ),
    )(
        *[
            pltpu.with_memory_space_constraint(v, pltpu.HBM)
            for v in (
                electric.reshape(3 * BX * BY, CZ),
                magnetic.reshape(3 * BX * BY, CZ),
                material.reshape(BX * BY, CZ),
                permittivity,
                source_cells.T,
                amplitudes.T,
                omegas,
                design_mask,
                forward_dft.reshape(BX * 6 * FREQ, 2 * LANES),
                pixel_anchor,
            )
        ]
    )
    adj, grad, fe = pl.pallas_call(
        deliver,
        out_shape=tuple(jax.ShapeDtypeStruct(v.shape, f32) for v in (adj, grad, fe)),
        in_specs=[anywhere] * 3,
        out_specs=(anywhere,) * 3,
        scratch_shapes=[pltpu.SemaphoreType.DMA((3,))],
        compiler_params=pltpu.CompilerParams(vmem_limit_bytes=1024 * 1024),
    )(adj, grad, fe)
    return adj.reshape(BX, 6 * FREQ, 2 * LANES), grad, fe.reshape(3, BX, BY, CZ)


def solution(mesh):
    return jax.shard_map(
        body_fn,
        mesh=mesh,
        in_specs=(
            P(None, "gx", "gy", "gz"),
            P(None, "gx", "gy", "gz"),
            P("gx", "gy", "gz"),
            P(),
            P(),
            P(),
            P(),
            P("gx", ("gy", "gz")),
            P("gx", None, ("gy", "gz")),
            P(),
        ),
        out_specs=(P("gx", None, ("gy", "gz")), P("gx", ("gy", "gz")), P(None, "gx", "gy", "gz")),
        check_vma=False,
    )
```

```python
import math

import jax
import jax.numpy as jnp
from jax import lax
from jax.experimental import pallas as pl
from jax.experimental.pallas import tpu as pltpu
from jax.sharding import PartitionSpec as P

SLAB = 32
FREQ = 4
MATS = 4
COURANT = 0.5

BX, BY, CZ = 8, 16, 48
HY = BY // 2
LANES = 128
DEPTH = 2 * CZ
BOTTOM = CZ // 4
COMPS = 7
ROWS = COMPS * BX
PAIRS = BY // 2
WIDE = 4
YY = HY + 2 * WIDE
SUB = 16


def roll(v, by, axis):
    return pltpu.roll(v, by % v.shape[axis], axis)


def iota(shape, axis):
    return lax.broadcasted_iota(jnp.int32, shape, axis)


def third(v):
    return (v * 21846) >> 16


def same_pixel(coord, anchor, by):
    shifted = coord + anchor
    place = shifted - 3 * third(shifted) + by
    return (place >= 0) & (place <= 2)


def kernel(
    e_in, h_in, mat_in, perm_in, cells_in, amps_in, omegas_in, mask_in, fwd_in, anchor_in,
    adj, grad, fe,
    perm, omegas, anchor,
    e_v, h_v, mat_v, cells_v, amps_v, mask_v, fwd_v, adj_v, coef_v,
    packed, edge, body0, body1, halo0, halo1, merged, fields, source, gain, flat,
    fe_send, fe_recv, sy, g_y, g_send, g_x,
    load_sem, send_sem, recv_sem,
):
    nx, ny = lax.axis_size("gx"), lax.axis_size("gy")
    gx, gy, core = lax.axis_index("gx"), lax.axis_index("gy"), lax.axis_index("gz")
    other = 1 - core
    up_x, down_x = lax.rem(gx + 1, nx), lax.rem(gx + nx - 1, nx)
    up_y, down_y = lax.rem(gy + 1, ny), lax.rem(gy + ny - 1, ny)

    barrier = pltpu.get_barrier_semaphore()
    face_y = jnp.where(core == 0, down_y, up_y)
    senders = [(x, face_y, h) for x in (up_x, down_x, gx) for h in (0, 1)]
    senders += [(x, gy, h) for x in (up_x, down_x) for h in (0, 1)] + [(gx, gy, other)]
    for sender in senders:
        pl.semaphore_signal(barrier, inc=1, device_id=sender, device_id_type=pl.DeviceIdType.MESH)

    loads = [
        pltpu.make_async_copy(src, dst, load_sem.at[i])
        for i, (src, dst) in enumerate(
            [(perm_in, perm), (mat_in, mat_v), (e_in, e_v), (h_in, h_v), (cells_in, cells_v), (amps_in, amps_v),
             (omegas_in, omegas), (anchor_in, anchor), (mask_in, mask_v)]
            + [(fwd_in.at[:, pl.ds(LANES * t, LANES)], fwd_v.at[t]) for t in (0, 1)]
        )
    ]
    for load in loads:
        load.start()

    edge[...] = jnp.zeros_like(edge)
    halo0[:, 16:48, :] = jnp.zeros((PAIRS, 32, LANES), jnp.float32)
    halo1[:, 16:48, :] = jnp.zeros((PAIRS - 2, 32, LANES), jnp.float32)

    for load in loads[:4]:
        load.wait()
    material = mat_v[...]
    eps = jnp.zeros(material.shape, jnp.float32)
    for level in range(MATS):
        eps = eps + jnp.where(material == level, perm[level], 0.0)
    coef_v[...] = COURANT / eps
    blank = jnp.zeros((ROWS, LANES - DEPTH), jnp.float32)
    for pair in range(PAIRS):
        rows = [
            jnp.concatenate(
                [
                    e_v[pl.ds(y, 3 * BX, stride=BY), :],
                    h_v[pl.ds(y, 3 * BX, stride=BY), :],
                    coef_v[pl.ds(y, BX, stride=BY), :],
                ],
                axis=0,
            )
            for y in (2 * pair, 2 * pair + 1)
        ]
        packed[pair] = jnp.concatenate(rows + [blank], axis=1)
    for pair in range(PAIRS):
        for side in (0, 1):
            for x in (0, 1):
                edge[side, pair, pl.ds(8 * x, COMPS), :] = packed[
                    pair, pl.ds((BX - 2) * side + x, COMPS, stride=BX), :
                ]
    for load in loads[4:]:
        load.wait()

    shape = (BX, LANES)
    r = iota(shape, 0)
    omega = jnp.zeros(shape, jnp.float32)
    for f in range(FREQ):
        omega = jnp.where((r & 3) == f, omegas[f], omega)
    phase = omega * ((r >> 2) + 1).astype(jnp.float32)
    cosine = jnp.cos(phase)
    sine = -jnp.sin(phase)
    square = omega * omega

    for t in (0, 1):
        lanes = pl.ds(LANES * t, LANES)
        design = 0.05 * mask_v[:, lanes].astype(jnp.float32)
        for c in range(3):
            gains = [jnp.zeros((BX, LANES), jnp.float32)] * 2
            for f in range(FREQ):
                real = square[f : f + 1, :] * fwd_v[t, pl.ds(3 * f + c, BX, stride=6 * FREQ), :]
                imag = square[f : f + 1, :] * fwd_v[t, pl.ds(3 * FREQ + 3 * f + c, BX, stride=6 * FREQ), :]
                for n in (0, 1):
                    k = FREQ * n + f
                    gains[n] = gains[n] + cosine[k : k + 1, :] * real - sine[k : k + 1, :] * imag
            for n in (0, 1):
                gain[n, c, :, lanes] = design * gains[n]

    lane_g = iota((BX, LANES), 1)
    firsts, lasts = [], []
    for n, c in ((0, 0), (0, 2), (1, 1)):
        one, two = gain[n, c], gain[n + (c == 2), (c + 1) % 3]
        firsts.append(jnp.where(lane_g < 64, one[:, :LANES], roll(two[:, :LANES], 64, 1)))
        lasts.append(jnp.where(lane_g < 64, roll(two[:, LANES:], 64, 1), one[:, LANES:]))
    for m in range(3):
        sy[0, m], sy[1, m] = firsts[m], lasts[m]

    def remote(src, dst, role, device):
        return pltpu.make_async_remote_copy(
            src_ref=src,
            dst_ref=dst,
            send_sem=send_sem.at[role[0]],
            recv_sem=recv_sem.at[role[1]],
            device_id=device,
            device_id_type=pl.DeviceIdType.MESH,
        )

    def sends_of(half):
        if half == 0:
            last, first, low, high = pl.ds(6, 2), pl.ds(0, 2), pl.ds(0, 6), pl.ds(2, 6)
            body, halo, at_low, at_high = body0, halo0, pl.ds(0, 2), pl.ds(6, 2)
            to_low, to_high = pl.ds(2, 6), pl.ds(0, 6)
        else:
            last, first, low, high = pl.ds(7, 1), pl.ds(0, 1), pl.ds(0, 5), pl.ds(3, 5)
            body, halo, at_low, at_high = body1, halo1, pl.ds(0, 1), pl.ds(5, 1)
            to_low, to_high = pl.ds(1, 5), pl.ds(0, 5)
        sides = ((0, down_x), (1, up_x))
        sends = []
        for side, to_x in sides:
            place = pl.ds(48 * side, 16)
            role = 7 + 2 * side + half
            sends += [
                remote(edge.at[side, last], halo.at[at_low, place], (3 + 4 * side, role), (to_x, up_y, 0)),
                remote(edge.at[side, first], halo.at[at_high, place], (4 + 4 * side, role), (to_x, down_y, 1)),
            ]
        sends += [
            remote(packed.at[last], body.at[at_low], (1, 1 + half), (gx, up_y, 0)),
            remote(packed.at[first], body.at[at_high], (2, 1 + half), (gx, down_y, 1)),
        ]
        for side, to_x in sides:
            place = pl.ds(48 * side, 16)
            role = 3 + 2 * side + half
            sends += [
                remote(edge.at[side, low], halo.at[to_low, place], (5 + 4 * side, role), (to_x, gy, 0)),
                remote(edge.at[side, high], halo.at[to_high, place], (6 + 4 * side, role), (to_x, gy, 1)),
            ]
        part, span = (high, to_high) if half == 0 else (low, to_low)
        sends.append(remote(packed.at[part], body.at[span], (0, 0), (gx, gy, 1 - half)))
        return sends

    above = (gx, jnp.where(core == 0, gy, up_y), other)
    below = (gx, jnp.where(core == 0, down_y, gy), other)
    beside = [remote(sy.at[0], g_y.at[0], (12, 12), below), remote(sy.at[1], g_y.at[1], (13, 13), above)]

    pl.semaphore_wait(barrier, len(senders))
    for half in (0, 1):
        @pl.when(core == half)
        def _(half=half):
            for send in sends_of(half):
                send.start()
            if half == 0:
                body0[2:8] = packed[0:6]
            else:
                body1[0:5] = packed[3:8]
    for send in beside:
        send.start()

    y_first = gy * BY + core * HY - WIDE
    row = iota((YY * SUB, 64), 0)
    sub = row & (SUB - 1)
    row_x = gx * BX + jnp.where(sub < 12, sub, sub - SUB)
    row_y = y_first + (row >> 4)
    hit = (row_x == cells_v[0:1, :]) & (row_y == cells_v[1:2, :])
    hit_z = jnp.where(iota((LANES, 64), 0) == cells_v[2:3, :], 1.0, 0.0)
    for c in range(3):
        left = jnp.where(hit, amps_v[c : c + 1, :], 0.0)
        source[c] = lax.dot_general(
            left, hit_z, (((1,), (1,)), ((), ())),
            precision=lax.Precision.HIGHEST, preferred_element_type=jnp.float32,
        ).reshape(YY, SUB, LANES)

    here = (gx, gy, other)
    for half in (0, 1):
        @pl.when(core != half)
        def _(half=half):
            if half == 0:
                remote(packed.at[pl.ds(2, 6)], body0.at[pl.ds(0, 6)], (0, 0), here).wait_recv()
            else:
                remote(packed.at[pl.ds(0, 5)], body1.at[pl.ds(1, 5)], (0, 0), here).wait_recv()

        body, halo = (body0, halo0) if half == 0 else (body1, halo1)
        face, long = (2, 6) if half == 0 else (1, 5)
        at_face = pl.ds(6 * core if half == 0 else 5 * core, face)
        span = pl.ds(2 - 2 * core if half == 0 else 1 - core, long)
        remote(packed.at[pl.ds(0, face)], body.at[at_face], (0, 1 + half), here).wait_recv()
        for side in (0, 1):
            place = pl.ds(48 * side, 16)
            x_part, corner = edge.at[0, pl.ds(0, long)], edge.at[0, pl.ds(0, face)]
            remote(x_part, halo.at[span, place], (0, 3 + 2 * side + half), here).wait_recv()
            remote(corner, halo.at[at_face, place], (0, 7 + 2 * side + half), here).wait_recv()

    x_of = iota((SUB, LANES), 0)
    x_of = gx * BX + jnp.where(x_of < 12, x_of, x_of - SUB)
    lane = iota((SUB, LANES), 1)
    inside = (x_of >= 0) & (x_of < nx * BX) & (lane < DEPTH)
    y_end = ny * BY

    lane_b = iota((ROWS, LANES), 1)
    lane_h = iota((64, LANES), 1)

    def merge(low, high, lanes):
        even = jnp.where(lanes < CZ, low, roll(high, CZ, 1))
        odd = jnp.where(lanes < CZ, roll(low, -CZ, 1), high)
        return even, odd

    for pair in range(YY // 2):
        if 1 <= pair <= PAIRS - 2:
            upper_own, upper_beside = body1[pair - 1], halo1[pair - 1]
        else:
            upper_own, upper_beside = jnp.zeros((ROWS, LANES), jnp.float32), jnp.zeros((64, LANES), jnp.float32)
        own = merge(body0[pair], upper_own, lane_b)
        edges = merge(halo0[pair], upper_beside, lane_h)
        for k in (0, 1):
            merged[k] = edges[k]
            yy = 2 * pair + k
            y = y_first + yy
            ok = inside & (y >= 0) & (y < y_end)
            for j in range(COMPS):
                tile = jnp.concatenate([own[k][BX * j : BX * j + BX], merged[k, pl.ds(j, 8, stride=8), :]], axis=0)
                fields[j, yy] = jnp.where(ok, tile, 0.0)

    half = jnp.where(inside, COURANT, 0.0)

    def magnetic_rows(first, last):
        def step(yy, carry):
            e0, e1, e2 = fields[0, yy], fields[1, yy], fields[2, yy]
            n0, n2 = fields[0, yy + 1], fields[2, yy + 1]
            y = y_first + yy
            scale = jnp.where((y >= 0) & (y < y_end), half, 0.0)
            fields[3, yy] = fields[3, yy] - scale * ((n2 - e2) - (roll(e1, -1, 1) - e1))
            fields[4, yy] = fields[4, yy] - scale * ((roll(e0, -1, 1) - e0) - (roll(e2, -1, 0) - e2))
            fields[5, yy] = fields[5, yy] - scale * ((roll(e1, -1, 0) - e1) - (n0 - e0))
            return carry

        lax.fori_loop(first, last, step, 0, unroll=True)

    def electric_rows(first, last, time):
        factor = math.cos(0.7 * (time + 0.5))

        def step(yy, carry):
            h0, h1, h2 = fields[3, yy], fields[4, yy], fields[5, yy]
            p0, p2 = fields[3, yy - 1], fields[5, yy - 1]
            scale = fields[6, yy]
            curls = (
                (h2 - p2) - (h1 - roll(h1, 1, 1)),
                (h0 - roll(h0, 1, 1)) - (h2 - roll(h2, 1, 0)),
                (h1 - roll(h1, 1, 0)) - (h0 - p0),
            )
            for c in range(3):
                fields[c, yy] = fields[c, yy] + scale * (curls[c] - factor * source[c, yy])
            return carry

        lax.fori_loop(first, last, step, 0, unroll=True)

    quarter = iota((BX, LANES), 1) >> 5

    def flatten(time):
        for c in range(3):
            for tile, first, quarters in ((0, 0, range(4)), (1, 4, range(4)), (2, 8, (0, 1)), (3, -4, (2, 3))):
                out = jnp.zeros((BX, LANES), jnp.float32)
                for q in quarters:
                    v = fields[c, WIDE + first + q, 0:BX, :]
                    out = jnp.where(quarter == q, roll(v, SLAB * q - BOTTOM, 1), out)
                flat[time, c, :, pl.ds(LANES * tile, LANES)] = out

    magnetic_rows(0, YY - 1)
    electric_rows(1, YY - 1, 0)
    flatten(0)
    magnetic_rows(1, YY - 2)
    electric_rows(2, YY - 2, 1)

    flatten(1)
    for send in beside:
        send.wait_recv()
    block = gy * 2 + core
    wide = (BX, 4 * LANES)
    total = jnp.zeros(wide, jnp.float32)
    for n in (0, 1):
        for c in range(3):
            k = 3 * n + c
            beyond = [roll(g_y[up, k // 2], 64, 1) if k % 2 else g_y[up, k // 2] for up in (0, 1)]
            total = total + jnp.concatenate([gain[n, c]] + beyond, axis=1) * flat[n, c]
    column = iota(wide, 1)
    y_ok = ((column < 3 * LANES) | (block > 0)) & ((column < 2 * LANES) | (column >= 3 * LANES) | (block < 2 * ny - 1))
    total = jnp.where(y_ok, total, 0.0)

    z = column & (SLAB - 1)
    along_z = total
    for by in (-2, -1, 1, 2):
        ok = same_pixel(z, anchor[2], by) & (z + by >= 0) & (z + by < SLAB)
        along_z = along_z + jnp.where(ok, roll(total, -by, 1), 0.0)
    shape = (BX, 2 * LANES)
    folded = along_z[:, : 2 * LANES]
    y_row = block * HY + (iota(shape, 1) >> 5)
    for by in (-2, -1, 1, 2):
        ok = same_pixel(y_row, anchor[1], by)
        folded = folded + jnp.where(ok, roll(along_z, -SLAB * by, 1)[:, : 2 * LANES], 0.0)
    g_send[...] = folded
    swaps = [
        remote(g_send, g_x.at[0], (14, 14), (down_x, gy, core)),
        remote(g_send, g_x.at[1], (15, 15), (up_x, gy, core)),
    ]
    for swap in swaps:
        swap.start()

    for y in range(HY):
        v = jnp.concatenate([fields[c, WIDE + y, 0:BX, :] for c in range(3)], axis=0)
        moved = roll(v, -CZ, 1)
        first = core == 0
        fe[pl.ds(HY * core + y, 3 * BX, stride=BY), :] = jnp.where(first, v, moved)[:, :CZ]
        fe_send[y] = jnp.where(first, moved, v)
    fe_copy = remote(fe_send, fe_recv, (11, 11), (gx, gy, other))
    fe_copy.start()

    for t in (0, 1):
        lanes = pl.ds(LANES * t, LANES)
        for f in range(FREQ):
            for p, weights in ((0, cosine), (1, sine)):
                for c in range(3):
                    rows = pl.ds(3 * FREQ * p + 3 * f + c, BX, stride=6 * FREQ)
                    adj_v[t, rows, :] = (
                        weights[f : f + 1, :] * flat[0, c, :, lanes]
                        + weights[FREQ + f : FREQ + f + 1, :] * flat[1, c, :, lanes]
                    )
    stores = [
        pltpu.make_async_copy(adj_v.at[t], adj.at[:, pl.ds(LANES * t, LANES)], load_sem.at[11 + t]) for t in (0, 1)
    ]
    for store in stores:
        store.start()

    fe_copy.wait_recv()
    for y in range(HY):
        fe[pl.ds(HY * other + y, 3 * BX, stride=BY), :] = fe_recv[y][:, :CZ]

    for swap in swaps:
        swap.wait_recv()
    x_row = iota(shape, 0)
    upper = jnp.where(gx < nx - 1, g_x[0], 0.0)
    lower = jnp.where(gx > 0, g_x[1], 0.0)
    extended = jnp.concatenate([folded, jnp.where(x_row < 4, upper, lower)], axis=0)
    result = folded
    for by in (-2, -1, 1, 2):
        ok = same_pixel(gx * BX + x_row, anchor[0], by)
        result = result + jnp.where(ok, roll(extended, -by, 0)[:BX], 0.0)
    grad[...] = result

    for half in (0, 1):
        @pl.when(core == half)
        def _(half=half):
            for send in sends_of(half):
                send.wait_send()
    for send in [fe_copy] + beside + swaps:
        send.wait_send()
    for store in stores:
        store.wait()


def deliver(adj, grad, fe, adj_out, grad_out, fe_out, sem):
    copies = [
        pltpu.make_async_copy(src, dst, sem.at[i])
        for i, (src, dst) in enumerate([(adj, adj_out), (fe, fe_out), (grad, grad_out)])
    ]
    for copy in copies:
        copy.start()
    for copy in copies:
        copy.wait()


def body_fn(
    electric, magnetic, material, permittivity, source_cells, amplitudes, omegas, design_mask, forward_dft, pixel_anchor
):
    f32 = jnp.float32
    anywhere = pl.BlockSpec(memory_space=pl.ANY)
    vmem = pl.BlockSpec(memory_space=pltpu.VMEM)
    adj, grad, fe = pl.pallas_call(
        kernel,
        out_shape=(
            jax.ShapeDtypeStruct((BX * 6 * FREQ, 2 * LANES), f32),
            jax.ShapeDtypeStruct((BX, 2 * LANES), f32),
            jax.ShapeDtypeStruct((3 * BX * BY, CZ), f32),
        ),
        in_specs=[anywhere] * 10,
        out_specs=(anywhere, vmem, vmem),
        scratch_shapes=[
            pltpu.SMEM((MATS,), f32),
            pltpu.SMEM((FREQ,), f32),
            pltpu.SMEM((3,), jnp.int32),
            pltpu.VMEM((3 * BX * BY, CZ), f32),
            pltpu.VMEM((3 * BX * BY, CZ), f32),
            pltpu.VMEM((BX * BY, CZ), jnp.int32),
            pltpu.VMEM((3, 64), jnp.int32),
            pltpu.VMEM((3, 64), f32),
            pltpu.VMEM((BX, 2 * LANES), jnp.int32),
            pltpu.VMEM((2, BX * 6 * FREQ, LANES), f32),
            pltpu.VMEM((2, BX * 6 * FREQ, LANES), f32),
            pltpu.VMEM((BX * BY, CZ), f32),
            pltpu.VMEM((PAIRS, ROWS, LANES), f32),
            pltpu.VMEM((2, PAIRS, 16, LANES), f32),
            pltpu.VMEM((PAIRS, ROWS, LANES), f32),
            pltpu.VMEM((PAIRS - 2, ROWS, LANES), f32),
            pltpu.VMEM((PAIRS, 64, LANES), f32),
            pltpu.VMEM((PAIRS - 2, 64, LANES), f32),
            pltpu.VMEM((2, 64, LANES), f32),
            pltpu.VMEM((COMPS, YY, SUB, LANES), f32),
            pltpu.VMEM((3, YY, SUB, LANES), f32),
            pltpu.VMEM((2, 3, BX, 2 * LANES), f32),
            pltpu.VMEM((2, 3, BX, 4 * LANES), f32),
            pltpu.VMEM((HY, 3 * BX, LANES), f32),
            pltpu.VMEM((HY, 3 * BX, LANES), f32),
            pltpu.VMEM((2, 3, BX, LANES), f32),
            pltpu.VMEM((2, 3, BX, LANES), f32),
            pltpu.VMEM((BX, 2 * LANES), f32),
            pltpu.VMEM((2, BX, 2 * LANES), f32),
            pltpu.SemaphoreType.DMA((13,)),
            pltpu.SemaphoreType.DMA((16,)),
            pltpu.SemaphoreType.DMA((16,)),
        ],
        compiler_params=pltpu.CompilerParams(
            collective_id=0, has_side_effects=True, vmem_limit_bytes=24 * 1024 * 1024
        ),
    )(
        *[
            pltpu.with_memory_space_constraint(v, pltpu.HBM)
            for v in (
                electric.reshape(3 * BX * BY, CZ),
                magnetic.reshape(3 * BX * BY, CZ),
                material.reshape(BX * BY, CZ),
                permittivity,
                source_cells.T,
                amplitudes.T,
                omegas,
                design_mask,
                forward_dft.reshape(BX * 6 * FREQ, 2 * LANES),
                pixel_anchor,
            )
        ]
    )
    adj, grad, fe = pl.pallas_call(
        deliver,
        out_shape=tuple(jax.ShapeDtypeStruct(v.shape, f32) for v in (adj, grad, fe)),
        in_specs=[anywhere] * 3,
        out_specs=(anywhere,) * 3,
        scratch_shapes=[pltpu.SemaphoreType.DMA((3,))],
        compiler_params=pltpu.CompilerParams(vmem_limit_bytes=1024 * 1024),
    )(adj, grad, fe)
    return adj.reshape(BX, 6 * FREQ, 2 * LANES), grad, fe.reshape(3, BX, BY, CZ)


def solution(mesh):
    return jax.shard_map(
        body_fn,
        mesh=mesh,
        in_specs=(
            P(None, "gx", "gy", "gz"),
            P(None, "gx", "gy", "gz"),
            P("gx", "gy", "gz"),
            P(),
            P(),
            P(),
            P(),
            P("gx", ("gy", "gz")),
            P("gx", None, ("gy", "gz")),
            P(),
        ),
        out_specs=(P("gx", None, ("gy", "gz")), P("gx", ("gy", "gz")), P(None, "gx", "gy", "gz")),
        check_vma=False,
    )
```

```python
import math

import jax
import jax.numpy as jnp
from jax import lax
from jax.experimental import pallas as pl
from jax.experimental.pallas import tpu as pltpu
from jax.sharding import PartitionSpec as P

SLAB = 32
FREQ = 4
MATS = 4
COURANT = 0.5

BX, BY, CZ = 8, 16, 48
HY = BY // 2
LANES = 128
DEPTH = 2 * CZ
BOTTOM = CZ // 4
COMPS = 7
ROWS = COMPS * BX
PAIRS = BY // 2
WIDE = 4
YY = HY + 2 * WIDE
SUB = 16


def roll(v, by, axis):
    return pltpu.roll(v, by % v.shape[axis], axis)


def iota(shape, axis):
    return lax.broadcasted_iota(jnp.int32, shape, axis)


def third(v):
    return (v * 21846) >> 16


def same_pixel(coord, anchor, by):
    shifted = coord + anchor
    place = shifted - 3 * third(shifted) + by
    return (place >= 0) & (place <= 2)


def kernel(
    e_in, h_in, mat_in, perm_in, cells_in, amps_in, omegas_in, mask_in, fwd_in, anchor_in,
    adj, grad, fe,
    perm, omegas, anchor,
    e_v, h_v, mat_v, cells_v, amps_v, mask_v, fwd_v, adj_v, coef_v,
    packed, edge, body0, body1, halo0, halo1, merged, fields, source, gain, flat,
    fe_send, fe_recv, sy, g_y, g_send, g_x,
    load_sem, send_sem, recv_sem,
):
    nx, ny = lax.axis_size("gx"), lax.axis_size("gy")
    gx, gy, core = lax.axis_index("gx"), lax.axis_index("gy"), lax.axis_index("gz")
    other = 1 - core
    up_x, down_x = lax.rem(gx + 1, nx), lax.rem(gx + nx - 1, nx)
    up_y, down_y = lax.rem(gy + 1, ny), lax.rem(gy + ny - 1, ny)

    barrier = pltpu.get_barrier_semaphore()
    face_y = jnp.where(core == 0, down_y, up_y)
    senders = [(x, face_y, h) for x in (up_x, down_x, gx) for h in (0, 1)]
    senders += [(x, gy, h) for x in (up_x, down_x) for h in (0, 1)] + [(gx, gy, other)]
    for sender in senders:
        pl.semaphore_signal(barrier, inc=1, device_id=sender, device_id_type=pl.DeviceIdType.MESH)

    loads = [
        pltpu.make_async_copy(src, dst, load_sem.at[i])
        for i, (src, dst) in enumerate(
            [(perm_in, perm), (mat_in, mat_v), (e_in, e_v), (h_in, h_v), (cells_in, cells_v), (amps_in, amps_v),
             (omegas_in, omegas), (anchor_in, anchor), (mask_in, mask_v)]
            + [(fwd_in.at[:, pl.ds(LANES * t, LANES)], fwd_v.at[t]) for t in (0, 1)]
        )
    ]
    for load in loads:
        load.start()

    edge[...] = jnp.zeros_like(edge)
    halo0[:, 16:48, :] = jnp.zeros((PAIRS, 32, LANES), jnp.float32)
    halo1[:, 16:48, :] = jnp.zeros((PAIRS - 2, 32, LANES), jnp.float32)

    for load in loads[:4]:
        load.wait()
    material = mat_v[...]
    eps = jnp.zeros(material.shape, jnp.float32)
    for level in range(MATS):
        eps = eps + jnp.where(material == level, perm[level], 0.0)
    coef_v[...] = COURANT / eps
    blank = jnp.zeros((ROWS, LANES - DEPTH), jnp.float32)
    for pair in range(PAIRS):
        rows = [
            jnp.concatenate(
                [
                    e_v[pl.ds(y, 3 * BX, stride=BY), :],
                    h_v[pl.ds(y, 3 * BX, stride=BY), :],
                    coef_v[pl.ds(y, BX, stride=BY), :],
                ],
                axis=0,
            )
            for y in (2 * pair, 2 * pair + 1)
        ]
        packed[pair] = jnp.concatenate(rows + [blank], axis=1)
    for pair in range(PAIRS):
        for side in (0, 1):
            for x in (0, 1):
                edge[side, pair, pl.ds(8 * x, COMPS), :] = packed[
                    pair, pl.ds((BX - 2) * side + x, COMPS, stride=BX), :
                ]
    for load in loads[4:]:
        load.wait()

    shape = (BX, LANES)
    r = iota(shape, 0)
    omega = jnp.zeros(shape, jnp.float32)
    for f in range(FREQ):
        omega = jnp.where((r & 3) == f, omegas[f], omega)
    phase = omega * ((r >> 2) + 1).astype(jnp.float32)
    cosine = jnp.cos(phase)
    sine = -jnp.sin(phase)
    square = omega * omega

    for t in (0, 1):
        lanes = pl.ds(LANES * t, LANES)
        design = 0.05 * mask_v[:, lanes].astype(jnp.float32)
        for c in range(3):
            gains = [jnp.zeros((BX, LANES), jnp.float32)] * 2
            for f in range(FREQ):
                real = square[f : f + 1, :] * fwd_v[t, pl.ds(3 * f + c, BX, stride=6 * FREQ), :]
                imag = square[f : f + 1, :] * fwd_v[t, pl.ds(3 * FREQ + 3 * f + c, BX, stride=6 * FREQ), :]
                for n in (0, 1):
                    k = FREQ * n + f
                    gains[n] = gains[n] + cosine[k : k + 1, :] * real - sine[k : k + 1, :] * imag
            for n in (0, 1):
                gain[n, c, :, lanes] = design * gains[n]

    lane_g = iota((BX, LANES), 1)
    firsts, lasts = [], []
    for n, c in ((0, 0), (0, 2), (1, 1)):
        one, two = gain[n, c], gain[n + (c == 2), (c + 1) % 3]
        firsts.append(jnp.where(lane_g < 64, one[:, :LANES], roll(two[:, :LANES], 64, 1)))
        lasts.append(jnp.where(lane_g < 64, roll(two[:, LANES:], 64, 1), one[:, LANES:]))
    for m in range(3):
        sy[0, m], sy[1, m] = firsts[m], lasts[m]

    def remote(src, dst, role, device):
        return pltpu.make_async_remote_copy(
            src_ref=src,
            dst_ref=dst,
            send_sem=send_sem.at[role[0]],
            recv_sem=recv_sem.at[role[1]],
            device_id=device,
            device_id_type=pl.DeviceIdType.MESH,
        )

    def sends_of(half):
        if half == 0:
            last, first, low, high = pl.ds(6, 2), pl.ds(0, 2), pl.ds(0, 6), pl.ds(2, 6)
            body, halo, at_low, at_high = body0, halo0, pl.ds(0, 2), pl.ds(6, 2)
            to_low, to_high = pl.ds(2, 6), pl.ds(0, 6)
        else:
            last, first, low, high = pl.ds(7, 1), pl.ds(0, 1), pl.ds(0, 5), pl.ds(3, 5)
            body, halo, at_low, at_high = body1, halo1, pl.ds(0, 1), pl.ds(5, 1)
            to_low, to_high = pl.ds(1, 5), pl.ds(0, 5)
        sides = ((0, down_x), (1, up_x))
        sends = []
        sends += [
            remote(packed.at[last], body.at[at_low], (1, 1 + half), (gx, up_y, 0)),
            remote(packed.at[first], body.at[at_high], (2, 1 + half), (gx, down_y, 1)),
        ]
        for side, to_x in sides:
            place = pl.ds(48 * side, 16)
            role = 7 + 2 * side + half
            sends += [
                remote(edge.at[side, last], halo.at[at_low, place], (3 + 4 * side, role), (to_x, up_y, 0)),
                remote(edge.at[side, first], halo.at[at_high, place], (4 + 4 * side, role), (to_x, down_y, 1)),
            ]
        for side, to_x in sides:
            place = pl.ds(48 * side, 16)
            role = 3 + 2 * side + half
            sends += [
                remote(edge.at[side, low], halo.at[to_low, place], (5 + 4 * side, role), (to_x, gy, 0)),
                remote(edge.at[side, high], halo.at[to_high, place], (6 + 4 * side, role), (to_x, gy, 1)),
            ]
        part, span = (high, to_high) if half == 0 else (low, to_low)
        sends.append(remote(packed.at[part], body.at[span], (0, 0), (gx, gy, 1 - half)))
        return sends

    above = (gx, jnp.where(core == 0, gy, up_y), other)
    below = (gx, jnp.where(core == 0, down_y, gy), other)
    beside = [remote(sy.at[0], g_y.at[0], (12, 12), below), remote(sy.at[1], g_y.at[1], (13, 13), above)]

    pl.semaphore_wait(barrier, len(senders))
    for send in beside:
        send.start()
    for half in (0, 1):
        @pl.when(core == half)
        def _(half=half):
            for send in sends_of(half):
                send.start()
            if half == 0:
                body0[2:8] = packed[0:6]
            else:
                body1[0:5] = packed[3:8]

    y_first = gy * BY + core * HY - WIDE
    row = iota((YY * SUB, 64), 0)
    sub = row & (SUB - 1)
    row_x = gx * BX + jnp.where(sub < 12, sub, sub - SUB)
    row_y = y_first + (row >> 4)
    hit = (row_x == cells_v[0:1, :]) & (row_y == cells_v[1:2, :])
    hit_z = jnp.where(iota((LANES, 64), 0) == cells_v[2:3, :], 1.0, 0.0)
    for c in range(3):
        left = jnp.where(hit, amps_v[c : c + 1, :], 0.0)
        source[c] = lax.dot_general(
            left, hit_z, (((1,), (1,)), ((), ())),
            precision=lax.Precision.HIGHEST, preferred_element_type=jnp.float32,
        ).reshape(YY, SUB, LANES)

    here = (gx, gy, other)
    for half in (0, 1):
        @pl.when(core != half)
        def _(half=half):
            if half == 0:
                remote(packed.at[pl.ds(2, 6)], body0.at[pl.ds(0, 6)], (0, 0), here).wait_recv()
            else:
                remote(packed.at[pl.ds(0, 5)], body1.at[pl.ds(1, 5)], (0, 0), here).wait_recv()

        body, halo = (body0, halo0) if half == 0 else (body1, halo1)
        face, long = (2, 6) if half == 0 else (1, 5)
        at_face = pl.ds(6 * core if half == 0 else 5 * core, face)
        span = pl.ds(2 - 2 * core if half == 0 else 1 - core, long)
        remote(packed.at[pl.ds(0, face)], body.at[at_face], (0, 1 + half), here).wait_recv()
        for side in (0, 1):
            place = pl.ds(48 * side, 16)
            x_part, corner = edge.at[0, pl.ds(0, long)], edge.at[0, pl.ds(0, face)]
            remote(x_part, halo.at[span, place], (0, 3 + 2 * side + half), here).wait_recv()
            remote(corner, halo.at[at_face, place], (0, 7 + 2 * side + half), here).wait_recv()

    x_of = iota((SUB, LANES), 0)
    x_of = gx * BX + jnp.where(x_of < 12, x_of, x_of - SUB)
    lane = iota((SUB, LANES), 1)
    inside = (x_of >= 0) & (x_of < nx * BX) & (lane < DEPTH)
    y_end = ny * BY

    lane_b = iota((ROWS, LANES), 1)
    lane_h = iota((64, LANES), 1)

    def merge(low, high, lanes):
        even = jnp.where(lanes < CZ, low, roll(high, CZ, 1))
        odd = jnp.where(lanes < CZ, roll(low, -CZ, 1), high)
        return even, odd

    for pair in range(YY // 2):
        if 1 <= pair <= PAIRS - 2:
            upper_own, upper_beside = body1[pair - 1], halo1[pair - 1]
        else:
            upper_own, upper_beside = jnp.zeros((ROWS, LANES), jnp.float32), jnp.zeros((64, LANES), jnp.float32)
        own = merge(body0[pair], upper_own, lane_b)
        edges = merge(halo0[pair], upper_beside, lane_h)
        for k in (0, 1):
            merged[k] = edges[k]
            yy = 2 * pair + k
            y = y_first + yy
            ok = inside & (y >= 0) & (y < y_end)
            for j in range(COMPS):
                tile = jnp.concatenate([own[k][BX * j : BX * j + BX], merged[k, pl.ds(j, 8, stride=8), :]], axis=0)
                fields[j, yy] = jnp.where(ok, tile, 0.0)

    half = jnp.where(inside, COURANT, 0.0)

    def magnetic_rows(first, last):
        def step(yy, carry):
            e0, e1, e2 = fields[0, yy], fields[1, yy], fields[2, yy]
            n0, n2 = fields[0, yy + 1], fields[2, yy + 1]
            y = y_first + yy
            scale = jnp.where((y >= 0) & (y < y_end), half, 0.0)
            fields[3, yy] = fields[3, yy] - scale * ((n2 - e2) - (roll(e1, -1, 1) - e1))
            fields[4, yy] = fields[4, yy] - scale * ((roll(e0, -1, 1) - e0) - (roll(e2, -1, 0) - e2))
            fields[5, yy] = fields[5, yy] - scale * ((roll(e1, -1, 0) - e1) - (n0 - e0))
            return carry

        lax.fori_loop(first, last, step, 0, unroll=True)

    def electric_rows(first, last, time):
        factor = math.cos(0.7 * (time + 0.5))

        def step(yy, carry):
            h0, h1, h2 = fields[3, yy], fields[4, yy], fields[5, yy]
            p0, p2 = fields[3, yy - 1], fields[5, yy - 1]
            scale = fields[6, yy]
            curls = (
                (h2 - p2) - (h1 - roll(h1, 1, 1)),
                (h0 - roll(h0, 1, 1)) - (h2 - roll(h2, 1, 0)),
                (h1 - roll(h1, 1, 0)) - (h0 - p0),
            )
            for c in range(3):
                fields[c, yy] = fields[c, yy] + scale * (curls[c] - factor * source[c, yy])
            return carry

        lax.fori_loop(first, last, step, 0, unroll=True)

    quarter = iota((BX, LANES), 1) >> 5

    def flatten(time):
        for c in range(3):
            for tile, first, quarters in ((0, 0, range(4)), (1, 4, range(4)), (2, 8, (0, 1)), (3, -4, (2, 3))):
                out = jnp.zeros((BX, LANES), jnp.float32)
                for q in quarters:
                    v = fields[c, WIDE + first + q, 0:BX, :]
                    out = jnp.where(quarter == q, roll(v, SLAB * q - BOTTOM, 1), out)
                flat[time, c, :, pl.ds(LANES * tile, LANES)] = out

    magnetic_rows(0, YY - 1)
    electric_rows(1, YY - 1, 0)
    flatten(0)
    magnetic_rows(1, YY - 2)
    electric_rows(2, YY - 2, 1)

    flatten(1)
    for send in beside:
        send.wait_recv()
    block = gy * 2 + core
    wide = (BX, 4 * LANES)
    total = jnp.zeros(wide, jnp.float32)
    for n in (0, 1):
        for c in range(3):
            k = 3 * n + c
            beyond = [roll(g_y[up, k // 2], 64, 1) if k % 2 else g_y[up, k // 2] for up in (0, 1)]
            total = total + jnp.concatenate([gain[n, c]] + beyond, axis=1) * flat[n, c]
    column = iota(wide, 1)
    y_ok = ((column < 3 * LANES) | (block > 0)) & ((column < 2 * LANES) | (column >= 3 * LANES) | (block < 2 * ny - 1))
    total = jnp.where(y_ok, total, 0.0)

    z = column & (SLAB - 1)
    along_z = total
    for by in (-2, -1, 1, 2):
        ok = same_pixel(z, anchor[2], by) & (z + by >= 0) & (z + by < SLAB)
        along_z = along_z + jnp.where(ok, roll(total, -by, 1), 0.0)
    shape = (BX, 2 * LANES)
    folded = along_z[:, : 2 * LANES]
    y_row = block * HY + (iota(shape, 1) >> 5)
    for by in (-2, -1, 1, 2):
        ok = same_pixel(y_row, anchor[1], by)
        folded = folded + jnp.where(ok, roll(along_z, -SLAB * by, 1)[:, : 2 * LANES], 0.0)
    g_send[...] = folded
    swaps = [
        remote(g_send, g_x.at[0], (14, 14), (down_x, gy, core)),
        remote(g_send, g_x.at[1], (15, 15), (up_x, gy, core)),
    ]
    for swap in swaps:
        swap.start()

    for y in range(HY):
        v = jnp.concatenate([fields[c, WIDE + y, 0:BX, :] for c in range(3)], axis=0)
        moved = roll(v, -CZ, 1)
        first = core == 0
        fe[pl.ds(HY * core + y, 3 * BX, stride=BY), :] = jnp.where(first, v, moved)[:, :CZ]
        fe_send[y] = jnp.where(first, moved, v)
    fe_copy = remote(fe_send, fe_recv, (11, 11), (gx, gy, other))
    fe_copy.start()

    for t in (0, 1):
        lanes = pl.ds(LANES * t, LANES)
        for f in range(FREQ):
            for p, weights in ((0, cosine), (1, sine)):
                for c in range(3):
                    rows = pl.ds(3 * FREQ * p + 3 * f + c, BX, stride=6 * FREQ)
                    adj_v[t, rows, :] = (
                        weights[f : f + 1, :] * flat[0, c, :, lanes]
                        + weights[FREQ + f : FREQ + f + 1, :] * flat[1, c, :, lanes]
                    )
    stores = [
        pltpu.make_async_copy(adj_v.at[t], adj.at[:, pl.ds(LANES * t, LANES)], load_sem.at[11 + t]) for t in (0, 1)
    ]
    for store in stores:
        store.start()

    fe_copy.wait_recv()
    for y in range(HY):
        fe[pl.ds(HY * other + y, 3 * BX, stride=BY), :] = fe_recv[y][:, :CZ]

    for swap in swaps:
        swap.wait_recv()
    x_row = iota(shape, 0)
    upper = jnp.where(gx < nx - 1, g_x[0], 0.0)
    lower = jnp.where(gx > 0, g_x[1], 0.0)
    extended = jnp.concatenate([folded, jnp.where(x_row < 4, upper, lower)], axis=0)
    result = folded
    for by in (-2, -1, 1, 2):
        ok = same_pixel(gx * BX + x_row, anchor[0], by)
        result = result + jnp.where(ok, roll(extended, -by, 0)[:BX], 0.0)
    grad[...] = result

    for half in (0, 1):
        @pl.when(core == half)
        def _(half=half):
            for send in sends_of(half):
                send.wait_send()
    for send in [fe_copy] + beside + swaps:
        send.wait_send()
    for store in stores:
        store.wait()


def deliver(adj, grad, fe, adj_out, grad_out, fe_out, sem):
    copies = [
        pltpu.make_async_copy(src, dst, sem.at[i])
        for i, (src, dst) in enumerate([(adj, adj_out), (fe, fe_out), (grad, grad_out)])
    ]
    for copy in copies:
        copy.start()
    for copy in copies:
        copy.wait()


def body_fn(
    electric, magnetic, material, permittivity, source_cells, amplitudes, omegas, design_mask, forward_dft, pixel_anchor
):
    f32 = jnp.float32
    anywhere = pl.BlockSpec(memory_space=pl.ANY)
    vmem = pl.BlockSpec(memory_space=pltpu.VMEM)
    adj, grad, fe = pl.pallas_call(
        kernel,
        out_shape=(
            jax.ShapeDtypeStruct((BX * 6 * FREQ, 2 * LANES), f32),
            jax.ShapeDtypeStruct((BX, 2 * LANES), f32),
            jax.ShapeDtypeStruct((3 * BX * BY, CZ), f32),
        ),
        in_specs=[anywhere] * 10,
        out_specs=(anywhere, vmem, vmem),
        scratch_shapes=[
            pltpu.SMEM((MATS,), f32),
            pltpu.SMEM((FREQ,), f32),
            pltpu.SMEM((3,), jnp.int32),
            pltpu.VMEM((3 * BX * BY, CZ), f32),
            pltpu.VMEM((3 * BX * BY, CZ), f32),
            pltpu.VMEM((BX * BY, CZ), jnp.int32),
            pltpu.VMEM((3, 64), jnp.int32),
            pltpu.VMEM((3, 64), f32),
            pltpu.VMEM((BX, 2 * LANES), jnp.int32),
            pltpu.VMEM((2, BX * 6 * FREQ, LANES), f32),
            pltpu.VMEM((2, BX * 6 * FREQ, LANES), f32),
            pltpu.VMEM((BX * BY, CZ), f32),
            pltpu.VMEM((PAIRS, ROWS, LANES), f32),
            pltpu.VMEM((2, PAIRS, 16, LANES), f32),
            pltpu.VMEM((PAIRS, ROWS, LANES), f32),
            pltpu.VMEM((PAIRS - 2, ROWS, LANES), f32),
            pltpu.VMEM((PAIRS, 64, LANES), f32),
            pltpu.VMEM((PAIRS - 2, 64, LANES), f32),
            pltpu.VMEM((2, 64, LANES), f32),
            pltpu.VMEM((COMPS, YY, SUB, LANES), f32),
            pltpu.VMEM((3, YY, SUB, LANES), f32),
            pltpu.VMEM((2, 3, BX, 2 * LANES), f32),
            pltpu.VMEM((2, 3, BX, 4 * LANES), f32),
            pltpu.VMEM((HY, 3 * BX, LANES), f32),
            pltpu.VMEM((HY, 3 * BX, LANES), f32),
            pltpu.VMEM((2, 3, BX, LANES), f32),
            pltpu.VMEM((2, 3, BX, LANES), f32),
            pltpu.VMEM((BX, 2 * LANES), f32),
            pltpu.VMEM((2, BX, 2 * LANES), f32),
            pltpu.SemaphoreType.DMA((13,)),
            pltpu.SemaphoreType.DMA((16,)),
            pltpu.SemaphoreType.DMA((16,)),
        ],
        compiler_params=pltpu.CompilerParams(
            collective_id=0, has_side_effects=True, vmem_limit_bytes=24 * 1024 * 1024
        ),
    )(
        *[
            pltpu.with_memory_space_constraint(v, pltpu.HBM)
            for v in (
                electric.reshape(3 * BX * BY, CZ),
                magnetic.reshape(3 * BX * BY, CZ),
                material.reshape(BX * BY, CZ),
                permittivity,
                source_cells.T,
                amplitudes.T,
                omegas,
                design_mask,
                forward_dft.reshape(BX * 6 * FREQ, 2 * LANES),
                pixel_anchor,
            )
        ]
    )
    adj, grad, fe = pl.pallas_call(
        deliver,
        out_shape=tuple(jax.ShapeDtypeStruct(v.shape, f32) for v in (adj, grad, fe)),
        in_specs=[anywhere] * 3,
        out_specs=(anywhere,) * 3,
        scratch_shapes=[pltpu.SemaphoreType.DMA((3,))],
        compiler_params=pltpu.CompilerParams(vmem_limit_bytes=1024 * 1024),
    )(adj, grad, fe)
    return adj.reshape(BX, 6 * FREQ, 2 * LANES), grad, fe.reshape(3, BX, BY, CZ)


def solution(mesh):
    return jax.shard_map(
        body_fn,
        mesh=mesh,
        in_specs=(
            P(None, "gx", "gy", "gz"),
            P(None, "gx", "gy", "gz"),
            P("gx", "gy", "gz"),
            P(),
            P(),
            P(),
            P(),
            P("gx", ("gy", "gz")),
            P("gx", None, ("gy", "gz")),
            P(),
        ),
        out_specs=(P("gx", None, ("gy", "gz")), P("gx", ("gy", "gz")), P(None, "gx", "gy", "gz")),
        check_vma=False,
    )
```

```python
import math

import jax
import jax.numpy as jnp
from jax import lax
from jax.experimental import pallas as pl
from jax.experimental.pallas import tpu as pltpu
from jax.sharding import PartitionSpec as P

SLAB = 32
FREQ = 4
MATS = 4
COURANT = 0.5

BX, BY, CZ = 8, 16, 48
HY = BY // 2
LANES = 128
DEPTH = 2 * CZ
BOTTOM = CZ // 4
COMPS = 7
ROWS = COMPS * BX
PAIRS = BY // 2
SENT = 5
YY = 12
SUB = 16


def roll(v, by, axis):
    return pltpu.roll(v, by % v.shape[axis], axis)


def iota(shape, axis):
    return lax.broadcasted_iota(jnp.int32, shape, axis)


def third(v):
    return (v * 21846) >> 16


def same_pixel(coord, anchor, by):
    shifted = coord + anchor
    place = shifted - 3 * third(shifted) + by
    return (place >= 0) & (place <= 2)


def kernel(
    e_in, h_in, mat_in, perm_in, cells_in, amps_in, omegas_in, mask_in, fwd_in, anchor_in,
    adj, grad, fe,
    perm, omegas, anchor,
    e_v, h_v, mat_v, cells_v, amps_v, mask_v, fwd_v, adj_v, coef_v,
    packed, edge, body, halo, merged, fields, source, gain, flat,
    fe_send, g_send, g_x, g_y, g_c,
    load_sem, send_sem, recv_sem,
):
    nx, ny = lax.axis_size("gx"), lax.axis_size("gy")
    gx, gy, core = lax.axis_index("gx"), lax.axis_index("gy"), lax.axis_index("gz")
    other = 1 - core
    up_x, down_x = lax.rem(gx + 1, nx), lax.rem(gx + nx - 1, nx)
    up_y, down_y = lax.rem(gy + 1, ny), lax.rem(gy + ny - 1, ny)

    barrier = pltpu.get_barrier_semaphore()
    face_y = jnp.where(core == 0, down_y, up_y)
    senders = [(x, face_y, h) for x in (up_x, down_x, gx) for h in (0, 1)]
    senders += [(x, gy, h) for x in (up_x, down_x) for h in (0, 1)] + [(gx, gy, other)]
    for sender in senders:
        pl.semaphore_signal(barrier, inc=1, device_id=sender, device_id_type=pl.DeviceIdType.MESH)

    loads = [
        pltpu.make_async_copy(src, dst, load_sem.at[i])
        for i, (src, dst) in enumerate(
            [(perm_in, perm), (mat_in, mat_v), (e_in, e_v), (h_in, h_v), (cells_in, cells_v), (amps_in, amps_v),
             (omegas_in, omegas), (anchor_in, anchor), (mask_in, mask_v)]
            + [(fwd_in.at[:, pl.ds(LANES * t, LANES)], fwd_v.at[t]) for t in (0, 1)]
        )
    ]
    for load in loads:
        load.start()

    edge[...] = jnp.zeros_like(edge)
    halo[:, :, 16:48, :] = jnp.zeros((2, YY // 2, 32, LANES), jnp.float32)

    for load in loads[:4]:
        load.wait()
    material = mat_v[...]
    eps = jnp.zeros(material.shape, jnp.float32)
    for level in range(MATS):
        eps = eps + jnp.where(material == level, perm[level], 0.0)
    coef_v[...] = COURANT / eps
    blank = jnp.zeros((ROWS, LANES - DEPTH), jnp.float32)
    for pair in range(PAIRS):
        rows = [
            jnp.concatenate(
                [
                    e_v[pl.ds(y, 3 * BX, stride=BY), :],
                    h_v[pl.ds(y, 3 * BX, stride=BY), :],
                    coef_v[pl.ds(y, BX, stride=BY), :],
                ],
                axis=0,
            )
            for y in (2 * pair, 2 * pair + 1)
        ]
        packed[pair] = jnp.concatenate(rows + [blank], axis=1)
    for pair in range(PAIRS):
        for side, first in ((0, 0), (1, BX - 2)):
            for x in (0, 1):
                edge[side, pair, pl.ds(8 * x, COMPS), :] = packed[
                    pair, pl.ds(first + x, COMPS, stride=BX), :
                ]

    def remote(src, dst, role, device):
        return pltpu.make_async_remote_copy(
            src_ref=src,
            dst_ref=dst,
            send_sem=send_sem.at[role[0]],
            recv_sem=recv_sem.at[role[1]],
            device_id=device,
            device_id_type=pl.DeviceIdType.MESH,
        )

    def part(dest):
        return packed.at[pl.ds(3 * dest, SENT)]

    def part_edge(side, dest):
        return edge.at[side, pl.ds(3 * dest, SENT)]

    def span(dest):
        return pl.ds(1 - dest, SENT)

    pl.semaphore_wait(barrier, len(senders))
    sends = []
    for side, to_x in ((0, down_x), (1, up_x)):
        place = pl.ds(48 * side, 16)
        sends += [
            remote(edge.at[side, PAIRS - 1], halo.at[core, 0, place], (3 + 4 * side, 7 + 2 * side + core), (to_x, up_y, 0)),
            remote(edge.at[side, 0], halo.at[core, 5, place], (4 + 4 * side, 7 + 2 * side + core), (to_x, down_y, 1)),
        ]
    sends += [
        remote(packed.at[PAIRS - 1], body.at[core, 0], (1, 1 + core), (gx, up_y, 0)),
        remote(packed.at[0], body.at[core, 5], (2, 1 + core), (gx, down_y, 1)),
    ]
    for side, to_x in ((0, down_x), (1, up_x)):
        place = pl.ds(48 * side, 16)
        for dest in (0, 1):
            sends.append(
                remote(part_edge(side, dest), halo.at[core, span(dest), place], (5 + 4 * side + dest, 3 + 2 * side + core), (to_x, gy, dest))
            )
    sends.append(remote(part(other), body.at[core, span(other)], (0, 0), (gx, gy, other)))
    for send in sends:
        send.start()

    body[core, span(core)] = packed[pl.ds(3 * core, SENT)]
    for load in loads[4:]:
        load.wait()

    y_first = gy * BY + core * HY - 2
    row = iota((YY * SUB, 64), 0)
    sub = row & (SUB - 1)
    row_x = gx * BX + jnp.where(sub < 12, sub, sub - SUB)
    row_y = y_first + (row >> 4)
    hit = (row_x == cells_v[0:1, :]) & (row_y == cells_v[1:2, :])
    hit_z = jnp.where(iota((LANES, 64), 0) == cells_v[2:3, :], 1.0, 0.0)
    for c in range(3):
        left = jnp.where(hit, amps_v[c : c + 1, :], 0.0)
        source[c] = lax.dot_general(
            left, hit_z, (((1,), (1,)), ((), ())),
            precision=lax.Precision.HIGHEST, preferred_element_type=jnp.float32,
        ).reshape(YY, SUB, LANES)

    shape = (BX, LANES)
    r = iota(shape, 0)
    omega = jnp.zeros(shape, jnp.float32)
    for f in range(FREQ):
        omega = jnp.where((r & 3) == f, omegas[f], omega)
    phase = omega * ((r >> 2) + 1).astype(jnp.float32)
    cosine = jnp.cos(phase)
    sine = -jnp.sin(phase)
    square = omega * omega

    for t in (0, 1):
        lanes = pl.ds(LANES * t, LANES)
        design = 0.05 * mask_v[:, lanes].astype(jnp.float32)
        for c in range(3):
            gains = [jnp.zeros((BX, LANES), jnp.float32)] * 2
            for f in range(FREQ):
                real = square[f : f + 1, :] * fwd_v[t, pl.ds(3 * f + c, BX, stride=6 * FREQ), :]
                imag = square[f : f + 1, :] * fwd_v[t, pl.ds(3 * FREQ + 3 * f + c, BX, stride=6 * FREQ), :]
                for n in (0, 1):
                    k = FREQ * n + f
                    gains[n] = gains[n] + cosine[k : k + 1, :] * real - sine[k : k + 1, :] * imag
            for n in (0, 1):
                gain[n, c, :, lanes] = design * gains[n]

    remote(part(core), body.at[other, span(core)], (0, 0), (gx, gy, other)).wait_recv()
    for h in (0, 1):
        remote(packed.at[0], body.at[h, 5 * core], (0, 1 + h), (gx, gy, other)).wait_recv()
        for side in (0, 1):
            place = pl.ds(48 * side, 16)
            remote(edge.at[0, pl.ds(0, SENT)], halo.at[h, span(core), place], (0, 3 + 2 * side + h), (gx, gy, other)).wait_recv()
            remote(edge.at[0, 0], halo.at[h, 5 * core, place], (0, 7 + 2 * side + h), (gx, gy, other)).wait_recv()

    x_of = iota((SUB, LANES), 0)
    x_of = gx * BX + jnp.where(x_of < 12, x_of, x_of - SUB)
    lane = iota((SUB, LANES), 1)
    inside = (x_of >= 0) & (x_of < nx * BX) & (lane < DEPTH)
    y_end = ny * BY

    lane_b = iota((ROWS, LANES), 1)
    lane_h = iota((64, LANES), 1)

    def merge(low, high, lanes):
        even = jnp.where(lanes < CZ, low, roll(high, CZ, 1))
        odd = jnp.where(lanes < CZ, roll(low, -CZ, 1), high)
        return even, odd

    for pair in range(YY // 2):
        own = merge(body[0, pair], body[1, pair], lane_b)
        beside = merge(halo[0, pair], halo[1, pair], lane_h)
        for k in (0, 1):
            merged[k] = beside[k]
            yy = 2 * pair + k
            y = y_first + yy
            ok = inside & (y >= 0) & (y < y_end)
            for j in range(COMPS):
                tile = jnp.concatenate([own[k][BX * j : BX * j + BX], merged[k, pl.ds(j, 8, stride=8), :]], axis=0)
                fields[j, yy] = jnp.where(ok, tile, 0.0)

    half = jnp.where(inside, COURANT, 0.0)

    def magnetic_rows(first, last):
        def step(yy, carry):
            e0, e1, e2 = fields[0, yy], fields[1, yy], fields[2, yy]
            n0, n2 = fields[0, yy + 1], fields[2, yy + 1]
            y = y_first + yy
            scale = jnp.where((y >= 0) & (y < y_end), half, 0.0)
            fields[3, yy] = fields[3, yy] - scale * ((n2 - e2) - (roll(e1, -1, 1) - e1))
            fields[4, yy] = fields[4, yy] - scale * ((roll(e0, -1, 1) - e0) - (roll(e2, -1, 0) - e2))
            fields[5, yy] = fields[5, yy] - scale * ((roll(e1, -1, 0) - e1) - (n0 - e0))
            return carry

        lax.fori_loop(first, last, step, 0, unroll=True)

    def electric_rows(first, last, time):
        factor = math.cos(0.7 * (time + 0.5))

        def step(yy, carry):
            h0, h1, h2 = fields[3, yy], fields[4, yy], fields[5, yy]
            p0, p2 = fields[3, yy - 1], fields[5, yy - 1]
            scale = fields[6, yy]
            curls = (
                (h2 - p2) - (h1 - roll(h1, 1, 1)),
                (h0 - roll(h0, 1, 1)) - (h2 - roll(h2, 1, 0)),
                (h1 - roll(h1, 1, 0)) - (h0 - p0),
            )
            for c in range(3):
                fields[c, yy] = fields[c, yy] + scale * (curls[c] - factor * source[c, yy])
            return carry

        lax.fori_loop(first, last, step, 0, unroll=True)

    quarter = iota((BX, LANES), 1) >> 5

    def flatten(time):
        for c in range(3):
            for tile in (0, 1):
                out = jnp.zeros((BX, LANES), jnp.float32)
                for q in range(4):
                    v = fields[c, 2 + 4 * tile + q, 0:BX, :]
                    out = jnp.where(quarter == q, roll(v, SLAB * q - BOTTOM, 1), out)
                flat[time, c, :, pl.ds(LANES * tile, LANES)] = out

    magnetic_rows(0, 11)
    electric_rows(1, 11, 0)
    flatten(0)
    magnetic_rows(1, 10)
    electric_rows(2, 10, 1)
    flatten(1)

    shape = (BX, 2 * LANES)
    total = jnp.zeros(shape, jnp.float32)
    for n in (0, 1):
        for c in range(3):
            total = total + gain[n, c] * flat[n, c]

    z = iota(shape, 1) & (SLAB - 1)
    folded = total
    for by in (-2, -1, 1, 2):
        ok = same_pixel(z, anchor[2], by) & (z + by >= 0) & (z + by < SLAB)
        folded = folded + jnp.where(ok, roll(total, -by, 1), 0.0)
    g_send[...] = folded

    above = (gx, jnp.where(core == 0, gy, up_y), other)
    below = (gx, jnp.where(core == 0, down_y, gy), other)
    first_rows, last_rows = g_send.at[:, pl.ds(0, LANES)], g_send.at[:, pl.ds(LANES, LANES)]
    swaps = [
        remote(first_rows, g_c.at[0, 0], (14, 14), (down_x,) + below[1:]),
        remote(last_rows, g_c.at[0, 1], (15, 15), (down_x,) + above[1:]),
        remote(first_rows, g_c.at[1, 0], (16, 16), (up_x,) + below[1:]),
        remote(last_rows, g_c.at[1, 1], (17, 17), (up_x,) + above[1:]),
        remote(first_rows, g_y.at[0], (12, 12), below),
        remote(last_rows, g_y.at[1], (13, 13), above),
        remote(g_send, g_x.at[0], (18, 18), (down_x, gy, core)),
        remote(g_send, g_x.at[1], (19, 19), (up_x, gy, core)),
    ]
    for swap in swaps:
        swap.start()

    fe_rows = fe.reshape(3 * BX * BY, CZ)
    for y in range(HY):
        v = jnp.concatenate([fields[c, 2 + y, 0:BX, :] for c in range(3)], axis=0)
        moved = roll(v, -CZ, 1)
        first = core == 0
        fe_rows[pl.ds(HY * core + y, 3 * BX, stride=BY), :] = jnp.where(first, v, moved)[:, :CZ]
        fe_send[pl.ds(y, 3 * BX, stride=HY), :] = jnp.where(first, moved, v)[:, :CZ]
    fe_copy = remote(
        fe_send.reshape(3 * BX, HY, CZ), fe.at[:, pl.ds(HY * core, HY), :], (11, 11), (gx, gy, other)
    )
    fe_copy.start()

    for t in (0, 1):
        lanes = pl.ds(LANES * t, LANES)
        for f in range(FREQ):
            for p, weights in ((0, cosine), (1, sine)):
                for c in range(3):
                    rows = pl.ds(3 * FREQ * p + 3 * f + c, BX, stride=6 * FREQ)
                    adj_v[t, rows, :] = (
                        weights[f : f + 1, :] * flat[0, c, :, lanes]
                        + weights[FREQ + f : FREQ + f + 1, :] * flat[1, c, :, lanes]
                    )
    stores = [
        pltpu.make_async_copy(adj_v.at[t], adj.at[:, pl.ds(LANES * t, LANES)], load_sem.at[11 + t]) for t in (0, 1)
    ]
    for store in stores:
        store.start()

    for swap in swaps:
        swap.wait_recv()
    block = gy * 2 + core
    wide = (BX, 4 * LANES)
    tile0 = jnp.concatenate([folded, g_y[0], g_y[1]], axis=1)
    upper = jnp.concatenate([g_x[0], g_c[0, 0], g_c[0, 1]], axis=1)
    lower = jnp.concatenate([g_x[1], g_c[1, 0], g_c[1, 1]], axis=1)
    x_row, column = iota(wide, 0), iota(wide, 1)
    upper = jnp.where(gx < nx - 1, upper, 0.0)
    lower = jnp.where(gx > 0, lower, 0.0)
    tile1 = jnp.where(x_row < 4, upper, lower)
    y_ok = (column < 2 * LANES) | ((column < 3 * LANES) & (block < 2 * ny - 1)) | ((column >= 3 * LANES) & (block > 0))
    extended = jnp.where(
        jnp.concatenate([y_ok, y_ok], axis=0), jnp.concatenate([tile0, tile1], axis=0), 0.0
    )
    along_x = extended[:BX]
    for by in (-2, -1, 1, 2):
        ok = same_pixel(gx * BX + x_row, anchor[0], by)
        along_x = along_x + jnp.where(ok, roll(extended, -by, 0)[:BX], 0.0)
    result = along_x[:, : 2 * LANES]
    y_row = block * HY + (iota(shape, 1) >> 5)
    for by in (-2, -1, 1, 2):
        ok = same_pixel(y_row, anchor[1], by)
        result = result + jnp.where(ok, roll(along_x, -SLAB * by, 1)[:, : 2 * LANES], 0.0)
    grad[...] = result
    remote(fe_send.reshape(3 * BX, HY, CZ), fe.at[:, pl.ds(HY * other, HY), :], (11, 11), (gx, gy, other)).wait_recv()

    for send in sends + [fe_copy] + swaps:
        send.wait_send()
    for store in stores:
        store.wait()


def deliver(adj, grad, fe, adj_out, grad_out, fe_out, sem):
    copies = [
        pltpu.make_async_copy(src, dst, sem.at[i])
        for i, (src, dst) in enumerate([(adj, adj_out), (fe, fe_out), (grad, grad_out)])
    ]
    for copy in copies:
        copy.start()
    for copy in copies:
        copy.wait()


def body_fn(
    electric, magnetic, material, permittivity, source_cells, amplitudes, omegas, design_mask, forward_dft, pixel_anchor
):
    f32 = jnp.float32
    anywhere = pl.BlockSpec(memory_space=pl.ANY)
    vmem = pl.BlockSpec(memory_space=pltpu.VMEM)
    adj, grad, fe = pl.pallas_call(
        kernel,
        out_shape=(
            jax.ShapeDtypeStruct((BX * 6 * FREQ, 2 * LANES), f32),
            jax.ShapeDtypeStruct((BX, 2 * LANES), f32),
            jax.ShapeDtypeStruct((3 * BX, BY, CZ), f32),
        ),
        in_specs=[anywhere] * 10,
        out_specs=(anywhere, vmem, vmem),
        scratch_shapes=[
            pltpu.SMEM((MATS,), f32),
            pltpu.SMEM((FREQ,), f32),
            pltpu.SMEM((3,), jnp.int32),
            pltpu.VMEM((3 * BX * BY, CZ), f32),
            pltpu.VMEM((3 * BX * BY, CZ), f32),
            pltpu.VMEM((BX * BY, CZ), jnp.int32),
            pltpu.VMEM((3, 64), jnp.int32),
            pltpu.VMEM((3, 64), f32),
            pltpu.VMEM((BX, 2 * LANES), jnp.int32),
            pltpu.VMEM((2, BX * 6 * FREQ, LANES), f32),
            pltpu.VMEM((2, BX * 6 * FREQ, LANES), f32),
            pltpu.VMEM((BX * BY, CZ), f32),
            pltpu.VMEM((PAIRS, ROWS, LANES), f32),
            pltpu.VMEM((2, PAIRS, 16, LANES), f32),
            pltpu.VMEM((2, YY // 2, ROWS, LANES), f32),
            pltpu.VMEM((2, YY // 2, 64, LANES), f32),
            pltpu.VMEM((2, 64, LANES), f32),
            pltpu.VMEM((COMPS, YY, SUB, LANES), f32),
            pltpu.VMEM((3, YY, SUB, LANES), f32),
            pltpu.VMEM((2, 3, BX, 2 * LANES), f32),
            pltpu.VMEM((2, 3, BX, 2 * LANES), f32),
            pltpu.VMEM((3 * BX * HY, CZ), f32),
            pltpu.VMEM((BX, 2 * LANES), f32),
            pltpu.VMEM((2, BX, 2 * LANES), f32),
            pltpu.VMEM((2, BX, LANES), f32),
            pltpu.VMEM((2, 2, BX, LANES), f32),
            pltpu.SemaphoreType.DMA((13,)),
            pltpu.SemaphoreType.DMA((20,)),
            pltpu.SemaphoreType.DMA((20,)),
        ],
        compiler_params=pltpu.CompilerParams(
            collective_id=0, has_side_effects=True, vmem_limit_bytes=24 * 1024 * 1024
        ),
    )(
        *[
            pltpu.with_memory_space_constraint(v, pltpu.HBM)
            for v in (
                electric.reshape(3 * BX * BY, CZ),
                magnetic.reshape(3 * BX * BY, CZ),
                material.reshape(BX * BY, CZ),
                permittivity,
                source_cells.T,
                amplitudes.T,
                omegas,
                design_mask,
                forward_dft.reshape(BX * 6 * FREQ, 2 * LANES),
                pixel_anchor,
            )
        ]
    )
    adj, grad, fe = pl.pallas_call(
        deliver,
        out_shape=tuple(jax.ShapeDtypeStruct(v.shape, f32) for v in (adj, grad, fe)),
        in_specs=[anywhere] * 3,
        out_specs=(anywhere,) * 3,
        scratch_shapes=[pltpu.SemaphoreType.DMA((3,))],
        compiler_params=pltpu.CompilerParams(vmem_limit_bytes=1024 * 1024),
    )(adj, grad, fe)
    return adj.reshape(BX, 6 * FREQ, 2 * LANES), grad, fe.reshape(3, BX, BY, CZ)


def solution(mesh):
    return jax.shard_map(
        body_fn,
        mesh=mesh,
        in_specs=(
            P(None, "gx", "gy", "gz"),
            P(None, "gx", "gy", "gz"),
            P("gx", "gy", "gz"),
            P(),
            P(),
            P(),
            P(),
            P("gx", ("gy", "gz")),
            P("gx", None, ("gy", "gz")),
            P(),
        ),
        out_specs=(P("gx", None, ("gy", "gz")), P("gx", ("gy", "gz")), P(None, "gx", "gy", "gz")),
        check_vma=False,
    )
```

```python
import math

import jax
import jax.numpy as jnp
from jax import lax
from jax.experimental import pallas as pl
from jax.experimental.pallas import tpu as pltpu
from jax.sharding import PartitionSpec as P

SLAB = 32
FREQ = 4
MATS = 4
COURANT = 0.5

BX, BY, CZ = 8, 16, 48
HY = BY // 2
LANES = 128
DEPTH = 2 * CZ
BOTTOM = CZ // 4
COMPS = 7
ROWS = COMPS * BX
PAIRS = BY // 2
SENT = 5
YY = 12
SUB = 16


def roll(v, by, axis):
    return pltpu.roll(v, by % v.shape[axis], axis)


def iota(shape, axis):
    return lax.broadcasted_iota(jnp.int32, shape, axis)


def third(v):
    return (v * 21846) >> 16


def same_pixel(coord, anchor, by):
    shifted = coord + anchor
    place = shifted - 3 * third(shifted) + by
    return (place >= 0) & (place <= 2)


def kernel(
    e_in, h_in, mat_in, perm_in, cells_in, amps_in, omegas_in, mask_in, fwd_in, anchor_in,
    adj, grad, fe,
    perm, omegas, anchor,
    e_v, h_v, mat_v, cells_v, amps_v, mask_v, fwd_v, adj_v, coef_v,
    packed, edge, body, halo, merged, fields, source, gain, flat,
    fe_send, fe_recv, g_send, g_x, g_y, g_c,
    load_sem, send_sem, recv_sem,
):
    nx, ny = lax.axis_size("gx"), lax.axis_size("gy")
    gx, gy, core = lax.axis_index("gx"), lax.axis_index("gy"), lax.axis_index("gz")
    other = 1 - core
    up_x, down_x = lax.rem(gx + 1, nx), lax.rem(gx + nx - 1, nx)
    up_y, down_y = lax.rem(gy + 1, ny), lax.rem(gy + ny - 1, ny)

    barrier = pltpu.get_barrier_semaphore()
    face_y = jnp.where(core == 0, down_y, up_y)
    senders = [(gx, gy, other)]
    for h in (0, 1):
        senders += [(up_x, gy, h), (down_x, gy, h)]
        senders += [(gx, face_y, h), (up_x, face_y, h), (down_x, face_y, h)]
    for sender in senders:
        pl.semaphore_signal(barrier, inc=1, device_id=sender, device_id_type=pl.DeviceIdType.MESH)

    loads = [
        pltpu.make_async_copy(src, dst, load_sem.at[i])
        for i, (src, dst) in enumerate(
            [(perm_in, perm), (mat_in, mat_v), (e_in, e_v), (h_in, h_v), (cells_in, cells_v), (amps_in, amps_v),
             (omegas_in, omegas), (anchor_in, anchor), (mask_in, mask_v)]
            + [(fwd_in.at[:, pl.ds(LANES * t, LANES)], fwd_v.at[t]) for t in (0, 1)]
        )
    ]
    for load in loads:
        load.start()

    edge[...] = jnp.zeros_like(edge)
    halo[:, :, 16:48, :] = jnp.zeros((2, YY // 2, 32, LANES), jnp.float32)

    for load in loads[:4]:
        load.wait()
    material = mat_v[...]
    eps = jnp.zeros(material.shape, jnp.float32)
    for level in range(MATS):
        eps = eps + jnp.where(material == level, perm[level], 0.0)
    coef_v[...] = COURANT / eps
    blank = jnp.zeros((ROWS, LANES - DEPTH), jnp.float32)
    for pair in range(PAIRS):
        rows = [
            jnp.concatenate(
                [
                    e_v[pl.ds(y, 3 * BX, stride=BY), :],
                    h_v[pl.ds(y, 3 * BX, stride=BY), :],
                    coef_v[pl.ds(y, BX, stride=BY), :],
                ],
                axis=0,
            )
            for y in (2 * pair, 2 * pair + 1)
        ]
        packed[pair] = jnp.concatenate(rows + [blank], axis=1)
    for pair in range(PAIRS):
        for side, first in ((0, 0), (1, BX - 2)):
            for x in (0, 1):
                edge[side, pair, pl.ds(8 * x, COMPS), :] = packed[
                    pair, pl.ds(first + x, COMPS, stride=BX), :
                ]

    def remote(src, dst, role, device):
        return pltpu.make_async_remote_copy(
            src_ref=src,
            dst_ref=dst,
            send_sem=send_sem.at[role[0]],
            recv_sem=recv_sem.at[role[1]],
            device_id=device,
            device_id_type=pl.DeviceIdType.MESH,
        )

    def part(dest):
        return packed.at[pl.ds(3 * dest, SENT)]

    def part_edge(side, dest):
        return edge.at[side, pl.ds(3 * dest, SENT)]

    def span(dest):
        return pl.ds(1 - dest, SENT)

    pl.semaphore_wait(barrier, len(senders))
    sends = [
        remote(packed.at[PAIRS - 1], body.at[core, 0], (1, 1 + core), (gx, up_y, 0)),
        remote(packed.at[0], body.at[core, 5], (2, 1 + core), (gx, down_y, 1)),
    ]
    for side, to_x in ((0, down_x), (1, up_x)):
        place = pl.ds(48 * side, 16)
        sends += [
            remote(edge.at[side, PAIRS - 1], halo.at[core, 0, place], (3 + 4 * side, 7 + 2 * side + core), (to_x, up_y, 0)),
            remote(edge.at[side, 0], halo.at[core, 5, place], (4 + 4 * side, 7 + 2 * side + core), (to_x, down_y, 1)),
        ]
    for side, to_x in ((0, down_x), (1, up_x)):
        place = pl.ds(48 * side, 16)
        for dest in (0, 1):
            sends.append(
                remote(part_edge(side, dest), halo.at[core, span(dest), place], (5 + 4 * side + dest, 3 + 2 * side + core), (to_x, gy, dest))
            )
    sends.append(remote(part(other), body.at[core, span(other)], (0, 0), (gx, gy, other)))
    for send in sends:
        send.start()

    body[core, span(core)] = packed[pl.ds(3 * core, SENT)]
    for load in loads[4:]:
        load.wait()

    y_first = gy * BY + core * HY - 2
    row = iota((YY * SUB, 64), 0)
    sub = row & (SUB - 1)
    row_x = gx * BX + jnp.where(sub < 12, sub, sub - SUB)
    row_y = y_first + (row >> 4)
    hit = (row_x == cells_v[0:1, :]) & (row_y == cells_v[1:2, :])
    hit_z = jnp.where(iota((LANES, 64), 0) == cells_v[2:3, :], 1.0, 0.0)
    for c in range(3):
        left = jnp.where(hit, amps_v[c : c + 1, :], 0.0)
        source[c] = lax.dot_general(
            left, hit_z, (((1,), (1,)), ((), ())),
            precision=lax.Precision.HIGHEST, preferred_element_type=jnp.float32,
        ).reshape(YY, SUB, LANES)

    shape = (BX, LANES)
    r = iota(shape, 0)
    omega = jnp.zeros(shape, jnp.float32)
    for f in range(FREQ):
        omega = jnp.where((r & 3) == f, omegas[f], omega)
    phase = omega * ((r >> 2) + 1).astype(jnp.float32)
    cosine = jnp.cos(phase)
    sine = -jnp.sin(phase)
    square = omega * omega

    for t in (0, 1):
        lanes = pl.ds(LANES * t, LANES)
        design = 0.05 * mask_v[:, lanes].astype(jnp.float32)
        for c in range(3):
            gains = [jnp.zeros((BX, LANES), jnp.float32)] * 2
            for f in range(FREQ):
                real = square[f : f + 1, :] * fwd_v[t, pl.ds(3 * f + c, BX, stride=6 * FREQ), :]
                imag = square[f : f + 1, :] * fwd_v[t, pl.ds(3 * FREQ + 3 * f + c, BX, stride=6 * FREQ), :]
                for n in (0, 1):
                    k = FREQ * n + f
                    gains[n] = gains[n] + cosine[k : k + 1, :] * real - sine[k : k + 1, :] * imag
            for n in (0, 1):
                gain[n, c, :, lanes] = design * gains[n]

    remote(part(core), body.at[other, span(core)], (0, 0), (gx, gy, other)).wait_recv()
    for h in (0, 1):
        for side in (0, 1):
            place = pl.ds(48 * side, 16)
            remote(edge.at[0, pl.ds(0, SENT)], halo.at[h, span(core), place], (0, 3 + 2 * side + h), (gx, gy, other)).wait_recv()

    x_of = iota((SUB, LANES), 0)
    x_of = gx * BX + jnp.where(x_of < 12, x_of, x_of - SUB)
    lane = iota((SUB, LANES), 1)
    inside = (x_of >= 0) & (x_of < nx * BX) & (lane < DEPTH)
    y_end = ny * BY

    lane_b = iota((ROWS, LANES), 1)
    lane_h = iota((64, LANES), 1)

    def merge(low, high, lanes):
        even = jnp.where(lanes < CZ, low, roll(high, CZ, 1))
        odd = jnp.where(lanes < CZ, roll(low, -CZ, 1), high)
        return even, odd

    def unpack(pair):
        own = merge(body[0, pair], body[1, pair], lane_b)
        beside = merge(halo[0, pair], halo[1, pair], lane_h)
        for k in (0, 1):
            merged[k] = beside[k]
            yy = 2 * pair + k
            y = y_first + yy
            ok = inside & (y >= 0) & (y < y_end)
            for j in range(COMPS):
                tile = jnp.concatenate([own[k][BX * j : BX * j + BX], merged[k, pl.ds(j, 8, stride=8), :]], axis=0)
                fields[j, yy] = jnp.where(ok, tile, 0.0)

    half = jnp.where(inside, COURANT, 0.0)

    def magnetic_rows(first, last):
        def step(yy, carry):
            e0, e1, e2 = fields[0, yy], fields[1, yy], fields[2, yy]
            n0, n2 = fields[0, yy + 1], fields[2, yy + 1]
            y = y_first + yy
            scale = jnp.where((y >= 0) & (y < y_end), half, 0.0)
            fields[3, yy] = fields[3, yy] - scale * ((n2 - e2) - (roll(e1, -1, 1) - e1))
            fields[4, yy] = fields[4, yy] - scale * ((roll(e0, -1, 1) - e0) - (roll(e2, -1, 0) - e2))
            fields[5, yy] = fields[5, yy] - scale * ((roll(e1, -1, 0) - e1) - (n0 - e0))
            return carry

        lax.fori_loop(first, last, step, 0, unroll=True)

    def electric_rows(first, last, time):
        factor = math.cos(0.7 * (time + 0.5))

        def step(yy, carry):
            h0, h1, h2 = fields[3, yy], fields[4, yy], fields[5, yy]
            p0, p2 = fields[3, yy - 1], fields[5, yy - 1]
            scale = fields[6, yy]
            curls = (
                (h2 - p2) - (h1 - roll(h1, 1, 1)),
                (h0 - roll(h0, 1, 1)) - (h2 - roll(h2, 1, 0)),
                (h1 - roll(h1, 1, 0)) - (h0 - p0),
            )
            for c in range(3):
                fields[c, yy] = fields[c, yy] + scale * (curls[c] - factor * source[c, yy])
            return carry

        lax.fori_loop(first, last, step, 0, unroll=True)

    quarter = iota((BX, LANES), 1) >> 5

    def flatten(time):
        for c in range(3):
            for tile in (0, 1):
                out = jnp.zeros((BX, LANES), jnp.float32)
                for q in range(4):
                    v = fields[c, 2 + 4 * tile + q, 0:BX, :]
                    out = jnp.where(quarter == q, roll(v, SLAB * q - BOTTOM, 1), out)
                flat[time, c, :, pl.ds(LANES * tile, LANES)] = out

    for pair in (1, 2, 3, 4):
        unpack(pair)
    magnetic_rows(2, 9)
    electric_rows(3, 9, 0)
    for h in (0, 1):
        remote(packed.at[0], body.at[h, 5 * core], (0, 1 + h), (gx, gy, other)).wait_recv()
        for side in (0, 1):
            place = pl.ds(48 * side, 16)
            remote(edge.at[0, 0], halo.at[h, 5 * core, place], (0, 7 + 2 * side + h), (gx, gy, other)).wait_recv()
    for pair in (0, 5):
        unpack(pair)
    magnetic_rows(0, 2)
    magnetic_rows(9, 11)
    electric_rows(1, 3, 0)
    electric_rows(9, 11, 0)
    flatten(0)
    magnetic_rows(1, 10)
    electric_rows(2, 10, 1)
    flatten(1)

    shape = (BX, 2 * LANES)
    total = jnp.zeros(shape, jnp.float32)
    for n in (0, 1):
        for c in range(3):
            total = total + gain[n, c] * flat[n, c]

    z = iota(shape, 1) & (SLAB - 1)
    folded = total
    for by in (-2, -1, 1, 2):
        ok = same_pixel(z, anchor[2], by) & (z + by >= 0) & (z + by < SLAB)
        folded = folded + jnp.where(ok, roll(total, -by, 1), 0.0)
    g_send[...] = folded

    above = (gx, jnp.where(core == 0, gy, up_y), other)
    below = (gx, jnp.where(core == 0, down_y, gy), other)
    first_rows, last_rows = g_send.at[:, pl.ds(0, LANES)], g_send.at[:, pl.ds(LANES, LANES)]
    swaps = [
        remote(first_rows, g_y.at[0], (12, 12), below),
        remote(last_rows, g_y.at[1], (13, 13), above),
        remote(first_rows, g_c.at[0, 0], (14, 14), (down_x,) + below[1:]),
        remote(last_rows, g_c.at[0, 1], (15, 15), (down_x,) + above[1:]),
        remote(first_rows, g_c.at[1, 0], (16, 16), (up_x,) + below[1:]),
        remote(last_rows, g_c.at[1, 1], (17, 17), (up_x,) + above[1:]),
        remote(g_send, g_x.at[0], (18, 18), (down_x, gy, core)),
        remote(g_send, g_x.at[1], (19, 19), (up_x, gy, core)),
    ]
    for swap in swaps:
        swap.start()

    for y in range(HY):
        v = jnp.concatenate([fields[c, 2 + y, 0:BX, :] for c in range(3)], axis=0)
        moved = roll(v, -CZ, 1)
        first = core == 0
        fe[pl.ds(HY * core + y, 3 * BX, stride=BY), :] = jnp.where(first, v, moved)[:, :CZ]
        fe_send[y] = jnp.where(first, moved, v)
    fe_copy = remote(fe_send, fe_recv, (11, 11), (gx, gy, other))
    fe_copy.start()

    for t in (0, 1):
        lanes = pl.ds(LANES * t, LANES)
        for f in range(FREQ):
            for p, weights in ((0, cosine), (1, sine)):
                for c in range(3):
                    rows = pl.ds(3 * FREQ * p + 3 * f + c, BX, stride=6 * FREQ)
                    adj_v[t, rows, :] = (
                        weights[f : f + 1, :] * flat[0, c, :, lanes]
                        + weights[FREQ + f : FREQ + f + 1, :] * flat[1, c, :, lanes]
                    )
    stores = [
        pltpu.make_async_copy(adj_v.at[t], adj.at[:, pl.ds(LANES * t, LANES)], load_sem.at[11 + t]) for t in (0, 1)
    ]
    for store in stores:
        store.start()

    fe_copy.wait_recv()
    for y in range(HY):
        fe[pl.ds(HY * other + y, 3 * BX, stride=BY), :] = fe_recv[y][:, :CZ]

    for swap in swaps:
        swap.wait_recv()
    block = gy * 2 + core
    wide = (BX, 4 * LANES)
    tile0 = jnp.concatenate([folded, g_y[0], g_y[1]], axis=1)
    upper = jnp.concatenate([g_x[0], g_c[0, 0], g_c[0, 1]], axis=1)
    lower = jnp.concatenate([g_x[1], g_c[1, 0], g_c[1, 1]], axis=1)
    x_row, column = iota(wide, 0), iota(wide, 1)
    upper = jnp.where(gx < nx - 1, upper, 0.0)
    lower = jnp.where(gx > 0, lower, 0.0)
    tile1 = jnp.where(x_row < 4, upper, lower)
    y_ok = (column < 2 * LANES) | ((column < 3 * LANES) & (block < 2 * ny - 1)) | ((column >= 3 * LANES) & (block > 0))
    extended = jnp.where(
        jnp.concatenate([y_ok, y_ok], axis=0), jnp.concatenate([tile0, tile1], axis=0), 0.0
    )
    along_x = extended[:BX]
    for by in (-2, -1, 1, 2):
        ok = same_pixel(gx * BX + x_row, anchor[0], by)
        along_x = along_x + jnp.where(ok, roll(extended, -by, 0)[:BX], 0.0)
    result = along_x[:, : 2 * LANES]
    y_row = block * HY + (iota(shape, 1) >> 5)
    for by in (-2, -1, 1, 2):
        ok = same_pixel(y_row, anchor[1], by)
        result = result + jnp.where(ok, roll(along_x, -SLAB * by, 1)[:, : 2 * LANES], 0.0)
    grad[...] = result

    for send in sends + [fe_copy] + swaps:
        send.wait_send()
    for store in stores:
        store.wait()


def deliver(adj, grad, fe, adj_out, grad_out, fe_out, sem):
    copies = [
        pltpu.make_async_copy(src, dst, sem.at[i])
        for i, (src, dst) in enumerate([(adj, adj_out), (fe, fe_out), (grad, grad_out)])
    ]
    for copy in copies:
        copy.start()
    for copy in copies:
        copy.wait()


def body_fn(
    electric, magnetic, material, permittivity, source_cells, amplitudes, omegas, design_mask, forward_dft, pixel_anchor
):
    f32 = jnp.float32
    anywhere = pl.BlockSpec(memory_space=pl.ANY)
    vmem = pl.BlockSpec(memory_space=pltpu.VMEM)
    adj, grad, fe = pl.pallas_call(
        kernel,
        out_shape=(
            jax.ShapeDtypeStruct((BX * 6 * FREQ, 2 * LANES), f32),
            jax.ShapeDtypeStruct((BX, 2 * LANES), f32),
            jax.ShapeDtypeStruct((3 * BX * BY, CZ), f32),
        ),
        in_specs=[anywhere] * 10,
        out_specs=(anywhere, vmem, vmem),
        scratch_shapes=[
            pltpu.SMEM((MATS,), f32),
            pltpu.SMEM((FREQ,), f32),
            pltpu.SMEM((3,), jnp.int32),
            pltpu.VMEM((3 * BX * BY, CZ), f32),
            pltpu.VMEM((3 * BX * BY, CZ), f32),
            pltpu.VMEM((BX * BY, CZ), jnp.int32),
            pltpu.VMEM((3, 64), jnp.int32),
            pltpu.VMEM((3, 64), f32),
            pltpu.VMEM((BX, 2 * LANES), jnp.int32),
            pltpu.VMEM((2, BX * 6 * FREQ, LANES), f32),
            pltpu.VMEM((2, BX * 6 * FREQ, LANES), f32),
            pltpu.VMEM((BX * BY, CZ), f32),
            pltpu.VMEM((PAIRS, ROWS, LANES), f32),
            pltpu.VMEM((2, PAIRS, 16, LANES), f32),
            pltpu.VMEM((2, YY // 2, ROWS, LANES), f32),
            pltpu.VMEM((2, YY // 2, 64, LANES), f32),
            pltpu.VMEM((2, 64, LANES), f32),
            pltpu.VMEM((COMPS, YY, SUB, LANES), f32),
            pltpu.VMEM((3, YY, SUB, LANES), f32),
            pltpu.VMEM((2, 3, BX, 2 * LANES), f32),
            pltpu.VMEM((2, 3, BX, 2 * LANES), f32),
            pltpu.VMEM((HY, 3 * BX, LANES), f32),
            pltpu.VMEM((HY, 3 * BX, LANES), f32),
            pltpu.VMEM((BX, 2 * LANES), f32),
            pltpu.VMEM((2, BX, 2 * LANES), f32),
            pltpu.VMEM((2, BX, LANES), f32),
            pltpu.VMEM((2, 2, BX, LANES), f32),
            pltpu.SemaphoreType.DMA((13,)),
            pltpu.SemaphoreType.DMA((20,)),
            pltpu.SemaphoreType.DMA((20,)),
        ],
        compiler_params=pltpu.CompilerParams(
            collective_id=0, has_side_effects=True, vmem_limit_bytes=24 * 1024 * 1024
        ),
    )(
        *[
            pltpu.with_memory_space_constraint(v, pltpu.HBM)
            for v in (
                electric.reshape(3 * BX * BY, CZ),
                magnetic.reshape(3 * BX * BY, CZ),
                material.reshape(BX * BY, CZ),
                permittivity,
                source_cells.T,
                amplitudes.T,
                omegas,
                design_mask,
                forward_dft.reshape(BX * 6 * FREQ, 2 * LANES),
                pixel_anchor,
            )
        ]
    )
    adj, grad, fe = pl.pallas_call(
        deliver,
        out_shape=tuple(jax.ShapeDtypeStruct(v.shape, f32) for v in (adj, grad, fe)),
        in_specs=[anywhere] * 3,
        out_specs=(anywhere,) * 3,
        scratch_shapes=[pltpu.SemaphoreType.DMA((3,))],
        compiler_params=pltpu.CompilerParams(vmem_limit_bytes=1024 * 1024),
    )(adj, grad, fe)
    return adj.reshape(BX, 6 * FREQ, 2 * LANES), grad, fe.reshape(3, BX, BY, CZ)


def solution(mesh):
    return jax.shard_map(
        body_fn,
        mesh=mesh,
        in_specs=(
            P(None, "gx", "gy", "gz"),
            P(None, "gx", "gy", "gz"),
            P("gx", "gy", "gz"),
            P(),
            P(),
            P(),
            P(),
            P("gx", ("gy", "gz")),
            P("gx", None, ("gy", "gz")),
            P(),
        ),
        out_specs=(P("gx", None, ("gy", "gz")), P("gx", ("gy", "gz")), P(None, "gx", "gy", "gz")),
        check_vma=False,
    )
```

```python
import math

import jax
import jax.numpy as jnp
from jax import lax
from jax.experimental import pallas as pl
from jax.experimental.pallas import tpu as pltpu
from jax.sharding import PartitionSpec as P

SLAB = 32
FREQ = 4
MATS = 4
COURANT = 0.5

BX, BY, CZ = 8, 16, 48
HY = BY // 2
LANES = 128
DEPTH = 2 * CZ
BOTTOM = CZ // 4
COMPS = 7
ROWS = COMPS * BX
PAIRS = BY // 2
SENT = 5
YY = 12
SUB = 16


def roll(v, by, axis):
    return pltpu.roll(v, by % v.shape[axis], axis)


def iota(shape, axis):
    return lax.broadcasted_iota(jnp.int32, shape, axis)


def third(v):
    return (v * 21846) >> 16


def same_pixel(coord, anchor, by):
    shifted = coord + anchor
    place = shifted - 3 * third(shifted) + by
    return (place >= 0) & (place <= 2)


def kernel(
    e_in, h_in, mat_in, perm_in, cells_in, amps_in, omegas_in, mask_in, fwd_in, anchor_in,
    adj, grad, fe,
    perm, omegas, anchor,
    e_v, h_v, mat_v, cells_v, amps_v, mask_v, fwd_v, adj_v, coef_v,
    packed, edge, body, halo, merged, fields, source, gain, flat,
    fe_send, fe_recv, g_send, g_x, g_y, g_c,
    load_sem, send_sem, recv_sem,
):
    nx, ny = lax.axis_size("gx"), lax.axis_size("gy")
    gx, gy, core = lax.axis_index("gx"), lax.axis_index("gy"), lax.axis_index("gz")
    other = 1 - core
    up_x, down_x = lax.rem(gx + 1, nx), lax.rem(gx + nx - 1, nx)
    up_y, down_y = lax.rem(gy + 1, ny), lax.rem(gy + ny - 1, ny)

    barrier = pltpu.get_barrier_semaphore()
    face_y = jnp.where(core == 0, down_y, up_y)
    senders = [(gx, gy, other)]
    for h in (0, 1):
        senders += [(up_x, gy, h), (down_x, gy, h)]
        senders += [(gx, face_y, h), (up_x, face_y, h), (down_x, face_y, h)]
    for sender in senders:
        pl.semaphore_signal(barrier, inc=1, device_id=sender, device_id_type=pl.DeviceIdType.MESH)

    loads = [
        pltpu.make_async_copy(src, dst, load_sem.at[i])
        for i, (src, dst) in enumerate(
            [(perm_in, perm), (mat_in, mat_v), (e_in, e_v), (h_in, h_v), (cells_in, cells_v), (amps_in, amps_v),
             (omegas_in, omegas), (anchor_in, anchor), (mask_in, mask_v)]
            + [(fwd_in.at[:, pl.ds(LANES * t, LANES)], fwd_v.at[t]) for t in (0, 1)]
        )
    ]
    for load in loads:
        load.start()

    edge[...] = jnp.zeros_like(edge)
    halo[:, :, 16:48, :] = jnp.zeros((2, YY // 2, 32, LANES), jnp.float32)

    halo[:, 5 * core, pl.ds(48 - 40 * core, 8), :] = jnp.zeros((2, 8, LANES), jnp.float32)

    for load in loads[:4]:
        load.wait()
    material = mat_v[...]
    eps = jnp.zeros(material.shape, jnp.float32)
    for level in range(MATS):
        eps = eps + jnp.where(material == level, perm[level], 0.0)
    coef_v[...] = COURANT / eps
    blank = jnp.zeros((ROWS, LANES - DEPTH), jnp.float32)
    for pair in range(PAIRS):
        rows = [
            jnp.concatenate(
                [
                    e_v[pl.ds(y, 3 * BX, stride=BY), :],
                    h_v[pl.ds(y, 3 * BX, stride=BY), :],
                    coef_v[pl.ds(y, BX, stride=BY), :],
                ],
                axis=0,
            )
            for y in (2 * pair, 2 * pair + 1)
        ]
        packed[pair] = jnp.concatenate(rows + [blank], axis=1)
    for pair in range(PAIRS):
        for side, first in ((0, 0), (1, BX - 2)):
            for x in (0, 1):
                edge[side, pair, pl.ds(8 * x, COMPS), :] = packed[
                    pair, pl.ds(first + x, COMPS, stride=BX), :
                ]

    def remote(src, dst, role, device):
        return pltpu.make_async_remote_copy(
            src_ref=src,
            dst_ref=dst,
            send_sem=send_sem.at[role[0]],
            recv_sem=recv_sem.at[role[1]],
            device_id=device,
            device_id_type=pl.DeviceIdType.MESH,
        )

    def part(dest):
        return packed.at[pl.ds(3 * dest, SENT)]

    def part_edge(side, dest):
        return edge.at[side, pl.ds(3 * dest, SENT)]

    def span(dest):
        return pl.ds(1 - dest, SENT)

    pl.semaphore_wait(barrier, len(senders))
    sends = [
        remote(packed.at[PAIRS - 1], body.at[core, 0], (1, 1 + core), (gx, up_y, 0)),
        remote(packed.at[0], body.at[core, 5], (2, 1 + core), (gx, down_y, 1)),
    ]
    for side, to_x in ((0, down_x), (1, up_x)):
        place = pl.ds(48 * side, 16)
        whole, near, near_place = pl.ds(0, 16), pl.ds(8 * side, 8), pl.ds(56 * side, 8)
        to_up, up_place = (near, near_place) if side == 1 else (whole, place)
        to_down, down_place = (near, near_place) if side == 0 else (whole, place)
        sends += [
            remote(edge.at[side, PAIRS - 1, to_up], halo.at[core, 0, up_place], (3 + 4 * side, 7 + 2 * side + core), (to_x, up_y, 0)),
            remote(edge.at[side, 0, to_down], halo.at[core, 5, down_place], (4 + 4 * side, 7 + 2 * side + core), (to_x, down_y, 1)),
        ]
    for side, to_x in ((0, down_x), (1, up_x)):
        place = pl.ds(48 * side, 16)
        for dest in (0, 1):
            sends.append(
                remote(part_edge(side, dest), halo.at[core, span(dest), place], (5 + 4 * side + dest, 3 + 2 * side + core), (to_x, gy, dest))
            )
    sends.append(remote(part(other), body.at[core, span(other)], (0, 0), (gx, gy, other)))
    for send in sends:
        send.start()

    body[core, span(core)] = packed[pl.ds(3 * core, SENT)]
    for load in loads[4:]:
        load.wait()

    y_first = gy * BY + core * HY - 2
    row = iota((YY * SUB, 64), 0)
    sub = row & (SUB - 1)
    row_x = gx * BX + jnp.where(sub < 12, sub, sub - SUB)
    row_y = y_first + (row >> 4)
    hit = (row_x == cells_v[0:1, :]) & (row_y == cells_v[1:2, :])
    hit_z = jnp.where(iota((LANES, 64), 0) == cells_v[2:3, :], 1.0, 0.0)
    for c in range(3):
        left = jnp.where(hit, amps_v[c : c + 1, :], 0.0)
        source[c] = lax.dot_general(
            left, hit_z, (((1,), (1,)), ((), ())),
            precision=lax.Precision.HIGHEST, preferred_element_type=jnp.float32,
        ).reshape(YY, SUB, LANES)

    shape = (BX, LANES)
    r = iota(shape, 0)
    omega = jnp.zeros(shape, jnp.float32)
    for f in range(FREQ):
        omega = jnp.where((r & 3) == f, omegas[f], omega)
    phase = omega * ((r >> 2) + 1).astype(jnp.float32)
    cosine = jnp.cos(phase)
    sine = -jnp.sin(phase)
    square = omega * omega

    for t in (0, 1):
        lanes = pl.ds(LANES * t, LANES)
        design = 0.05 * mask_v[:, lanes].astype(jnp.float32)
        for c in range(3):
            gains = [jnp.zeros((BX, LANES), jnp.float32)] * 2
            for f in range(FREQ):
                real = square[f : f + 1, :] * fwd_v[t, pl.ds(3 * f + c, BX, stride=6 * FREQ), :]
                imag = square[f : f + 1, :] * fwd_v[t, pl.ds(3 * FREQ + 3 * f + c, BX, stride=6 * FREQ), :]
                for n in (0, 1):
                    k = FREQ * n + f
                    gains[n] = gains[n] + cosine[k : k + 1, :] * real - sine[k : k + 1, :] * imag
            for n in (0, 1):
                gain[n, c, :, lanes] = design * gains[n]

    remote(part(core), body.at[other, span(core)], (0, 0), (gx, gy, other)).wait_recv()
    for h in (0, 1):
        remote(packed.at[0], body.at[h, 5 * core], (0, 1 + h), (gx, gy, other)).wait_recv()
        for side in (0, 1):
            place = pl.ds(48 * side, 16)
            remote(edge.at[0, pl.ds(0, SENT)], halo.at[h, span(core), place], (0, 3 + 2 * side + h), (gx, gy, other)).wait_recv()
            for c, rows, at in ((side, 16, 48 * side), (1 - side, 8, 56 * side)):
                @pl.when(core == c)
                def _(h=h, side=side, c=c, rows=rows, at=at):
                    remote(
                        edge.at[0, 0, pl.ds(0, rows)], halo.at[h, 5 * c, pl.ds(at, rows)], (0, 7 + 2 * side + h), (gx, gy, other)
                    ).wait_recv()

    x_of = iota((SUB, LANES), 0)
    x_of = gx * BX + jnp.where(x_of < 12, x_of, x_of - SUB)
    lane = iota((SUB, LANES), 1)
    inside = (x_of >= 0) & (x_of < nx * BX) & (lane < DEPTH)
    y_end = ny * BY

    lane_b = iota((ROWS, LANES), 1)
    lane_h = iota((64, LANES), 1)

    def merge(low, high, lanes):
        even = jnp.where(lanes < CZ, low, roll(high, CZ, 1))
        odd = jnp.where(lanes < CZ, roll(low, -CZ, 1), high)
        return even, odd

    for pair in range(YY // 2):
        own = merge(body[0, pair], body[1, pair], lane_b)
        beside = merge(halo[0, pair], halo[1, pair], lane_h)
        for k in (0, 1):
            merged[k] = beside[k]
            yy = 2 * pair + k
            y = y_first + yy
            ok = inside & (y >= 0) & (y < y_end)
            for j in range(COMPS):
                tile = jnp.concatenate([own[k][BX * j : BX * j + BX], merged[k, pl.ds(j, 8, stride=8), :]], axis=0)
                fields[j, yy] = jnp.where(ok, tile, 0.0)

    half = jnp.where(inside, COURANT, 0.0)

    def magnetic_rows(first, last):
        def step(yy, carry):
            e0, e1, e2 = fields[0, yy], fields[1, yy], fields[2, yy]
            n0, n2 = fields[0, yy + 1], fields[2, yy + 1]
            y = y_first + yy
            scale = jnp.where((y >= 0) & (y < y_end), half, 0.0)
            fields[3, yy] = fields[3, yy] - scale * ((n2 - e2) - (roll(e1, -1, 1) - e1))
            fields[4, yy] = fields[4, yy] - scale * ((roll(e0, -1, 1) - e0) - (roll(e2, -1, 0) - e2))
            fields[5, yy] = fields[5, yy] - scale * ((roll(e1, -1, 0) - e1) - (n0 - e0))
            return carry

        lax.fori_loop(first, last, step, 0, unroll=True)

    def electric_rows(first, last, time):
        factor = math.cos(0.7 * (time + 0.5))

        def step(yy, carry):
            h0, h1, h2 = fields[3, yy], fields[4, yy], fields[5, yy]
            p0, p2 = fields[3, yy - 1], fields[5, yy - 1]
            scale = fields[6, yy]
            curls = (
                (h2 - p2) - (h1 - roll(h1, 1, 1)),
                (h0 - roll(h0, 1, 1)) - (h2 - roll(h2, 1, 0)),
                (h1 - roll(h1, 1, 0)) - (h0 - p0),
            )
            for c in range(3):
                fields[c, yy] = fields[c, yy] + scale * (curls[c] - factor * source[c, yy])
            return carry

        lax.fori_loop(first, last, step, 0, unroll=True)

    quarter = iota((BX, LANES), 1) >> 5

    def flatten(time):
        for c in range(3):
            for tile in (0, 1):
                out = jnp.zeros((BX, LANES), jnp.float32)
                for q in range(4):
                    v = fields[c, 2 + 4 * tile + q, 0:BX, :]
                    out = jnp.where(quarter == q, roll(v, SLAB * q - BOTTOM, 1), out)
                flat[time, c, :, pl.ds(LANES * tile, LANES)] = out

    magnetic_rows(0, 11)
    electric_rows(1, 11, 0)
    flatten(0)
    magnetic_rows(1, 10)
    electric_rows(2, 10, 1)
    flatten(1)

    shape = (BX, 2 * LANES)
    total = jnp.zeros(shape, jnp.float32)
    for n in (0, 1):
        for c in range(3):
            total = total + gain[n, c] * flat[n, c]

    z = iota(shape, 1) & (SLAB - 1)
    folded = total
    for by in (-2, -1, 1, 2):
        ok = same_pixel(z, anchor[2], by) & (z + by >= 0) & (z + by < SLAB)
        folded = folded + jnp.where(ok, roll(total, -by, 1), 0.0)
    g_send[...] = folded

    above = (gx, jnp.where(core == 0, gy, up_y), other)
    below = (gx, jnp.where(core == 0, down_y, gy), other)
    first_rows, last_rows = g_send.at[:, pl.ds(0, LANES)], g_send.at[:, pl.ds(LANES, LANES)]
    swaps = [
        remote(first_rows, g_y.at[0], (12, 12), below),
        remote(last_rows, g_y.at[1], (13, 13), above),
        remote(first_rows, g_c.at[0, 0], (14, 14), (down_x,) + below[1:]),
        remote(last_rows, g_c.at[0, 1], (15, 15), (down_x,) + above[1:]),
        remote(first_rows, g_c.at[1, 0], (16, 16), (up_x,) + below[1:]),
        remote(last_rows, g_c.at[1, 1], (17, 17), (up_x,) + above[1:]),
        remote(g_send, g_x.at[0], (18, 18), (down_x, gy, core)),
        remote(g_send, g_x.at[1], (19, 19), (up_x, gy, core)),
    ]
    for swap in swaps:
        swap.start()

    for y in range(HY):
        v = jnp.concatenate([fields[c, 2 + y, 0:BX, :] for c in range(3)], axis=0)
        moved = roll(v, -CZ, 1)
        first = core == 0
        fe[pl.ds(HY * core + y, 3 * BX, stride=BY), :] = jnp.where(first, v, moved)[:, :CZ]
        fe_send[y] = jnp.where(first, moved, v)
    fe_copy = remote(fe_send, fe_recv, (11, 11), (gx, gy, other))
    fe_copy.start()

    for t in (0, 1):
        lanes = pl.ds(LANES * t, LANES)
        for f in range(FREQ):
            for p, weights in ((0, cosine), (1, sine)):
                for c in range(3):
                    rows = pl.ds(3 * FREQ * p + 3 * f + c, BX, stride=6 * FREQ)
                    adj_v[t, rows, :] = (
                        weights[f : f + 1, :] * flat[0, c, :, lanes]
                        + weights[FREQ + f : FREQ + f + 1, :] * flat[1, c, :, lanes]
                    )
    stores = [
        pltpu.make_async_copy(adj_v.at[t], adj.at[:, pl.ds(LANES * t, LANES)], load_sem.at[11 + t]) for t in (0, 1)
    ]
    for store in stores:
        store.start()

    fe_copy.wait_recv()
    for y in range(HY):
        fe[pl.ds(HY * other + y, 3 * BX, stride=BY), :] = fe_recv[y][:, :CZ]

    for swap in swaps:
        swap.wait_recv()
    block = gy * 2 + core
    wide = (BX, 4 * LANES)
    tile0 = jnp.concatenate([folded, g_y[0], g_y[1]], axis=1)
    upper = jnp.concatenate([g_x[0], g_c[0, 0], g_c[0, 1]], axis=1)
    lower = jnp.concatenate([g_x[1], g_c[1, 0], g_c[1, 1]], axis=1)
    x_row, column = iota(wide, 0), iota(wide, 1)
    upper = jnp.where(gx < nx - 1, upper, 0.0)
    lower = jnp.where(gx > 0, lower, 0.0)
    tile1 = jnp.where(x_row < 4, upper, lower)
    y_ok = (column < 2 * LANES) | ((column < 3 * LANES) & (block < 2 * ny - 1)) | ((column >= 3 * LANES) & (block > 0))
    extended = jnp.where(
        jnp.concatenate([y_ok, y_ok], axis=0), jnp.concatenate([tile0, tile1], axis=0), 0.0
    )
    along_x = extended[:BX]
    for by in (-2, -1, 1, 2):
        ok = same_pixel(gx * BX + x_row, anchor[0], by)
        along_x = along_x + jnp.where(ok, roll(extended, -by, 0)[:BX], 0.0)
    result = along_x[:, : 2 * LANES]
    y_row = block * HY + (iota(shape, 1) >> 5)
    for by in (-2, -1, 1, 2):
        ok = same_pixel(y_row, anchor[1], by)
        result = result + jnp.where(ok, roll(along_x, -SLAB * by, 1)[:, : 2 * LANES], 0.0)
    grad[...] = result

    for send in sends + [fe_copy] + swaps:
        send.wait_send()
    for store in stores:
        store.wait()


def deliver(adj, grad, fe, adj_out, grad_out, fe_out, sem):
    copies = [
        pltpu.make_async_copy(src, dst, sem.at[i])
        for i, (src, dst) in enumerate([(adj, adj_out), (fe, fe_out), (grad, grad_out)])
    ]
    for copy in copies:
        copy.start()
    for copy in copies:
        copy.wait()


def body_fn(
    electric, magnetic, material, permittivity, source_cells, amplitudes, omegas, design_mask, forward_dft, pixel_anchor
):
    f32 = jnp.float32
    anywhere = pl.BlockSpec(memory_space=pl.ANY)
    vmem = pl.BlockSpec(memory_space=pltpu.VMEM)
    adj, grad, fe = pl.pallas_call(
        kernel,
        out_shape=(
            jax.ShapeDtypeStruct((BX * 6 * FREQ, 2 * LANES), f32),
            jax.ShapeDtypeStruct((BX, 2 * LANES), f32),
            jax.ShapeDtypeStruct((3 * BX * BY, CZ), f32),
        ),
        in_specs=[anywhere] * 10,
        out_specs=(anywhere, vmem, vmem),
        scratch_shapes=[
            pltpu.SMEM((MATS,), f32),
            pltpu.SMEM((FREQ,), f32),
            pltpu.SMEM((3,), jnp.int32),
            pltpu.VMEM((3 * BX * BY, CZ), f32),
            pltpu.VMEM((3 * BX * BY, CZ), f32),
            pltpu.VMEM((BX * BY, CZ), jnp.int32),
            pltpu.VMEM((3, 64), jnp.int32),
            pltpu.VMEM((3, 64), f32),
            pltpu.VMEM((BX, 2 * LANES), jnp.int32),
            pltpu.VMEM((2, BX * 6 * FREQ, LANES), f32),
            pltpu.VMEM((2, BX * 6 * FREQ, LANES), f32),
            pltpu.VMEM((BX * BY, CZ), f32),
            pltpu.VMEM((PAIRS, ROWS, LANES), f32),
            pltpu.VMEM((2, PAIRS, 16, LANES), f32),
            pltpu.VMEM((2, YY // 2, ROWS, LANES), f32),
            pltpu.VMEM((2, YY // 2, 64, LANES), f32),
            pltpu.VMEM((2, 64, LANES), f32),
            pltpu.VMEM((COMPS, YY, SUB, LANES), f32),
            pltpu.VMEM((3, YY, SUB, LANES), f32),
            pltpu.VMEM((2, 3, BX, 2 * LANES), f32),
            pltpu.VMEM((2, 3, BX, 2 * LANES), f32),
            pltpu.VMEM((HY, 3 * BX, LANES), f32),
            pltpu.VMEM((HY, 3 * BX, LANES), f32),
            pltpu.VMEM((BX, 2 * LANES), f32),
            pltpu.VMEM((2, BX, 2 * LANES), f32),
            pltpu.VMEM((2, BX, LANES), f32),
            pltpu.VMEM((2, 2, BX, LANES), f32),
            pltpu.SemaphoreType.DMA((13,)),
            pltpu.SemaphoreType.DMA((20,)),
            pltpu.SemaphoreType.DMA((20,)),
        ],
        compiler_params=pltpu.CompilerParams(
            collective_id=0, has_side_effects=True, vmem_limit_bytes=24 * 1024 * 1024
        ),
    )(
        *[
            pltpu.with_memory_space_constraint(v, pltpu.HBM)
            for v in (
                electric.reshape(3 * BX * BY, CZ),
                magnetic.reshape(3 * BX * BY, CZ),
                material.reshape(BX * BY, CZ),
                permittivity,
                source_cells.T,
                amplitudes.T,
                omegas,
                design_mask,
                forward_dft.reshape(BX * 6 * FREQ, 2 * LANES),
                pixel_anchor,
            )
        ]
    )
    adj, grad, fe = pl.pallas_call(
        deliver,
        out_shape=tuple(jax.ShapeDtypeStruct(v.shape, f32) for v in (adj, grad, fe)),
        in_specs=[anywhere] * 3,
        out_specs=(anywhere,) * 3,
        scratch_shapes=[pltpu.SemaphoreType.DMA((3,))],
        compiler_params=pltpu.CompilerParams(vmem_limit_bytes=1024 * 1024),
    )(adj, grad, fe)
    return adj.reshape(BX, 6 * FREQ, 2 * LANES), grad, fe.reshape(3, BX, BY, CZ)


def solution(mesh):
    return jax.shard_map(
        body_fn,
        mesh=mesh,
        in_specs=(
            P(None, "gx", "gy", "gz"),
            P(None, "gx", "gy", "gz"),
            P("gx", "gy", "gz"),
            P(),
            P(),
            P(),
            P(),
            P("gx", ("gy", "gz")),
            P("gx", None, ("gy", "gz")),
            P(),
        ),
        out_specs=(P("gx", None, ("gy", "gz")), P("gx", ("gy", "gz")), P(None, "gx", "gy", "gz")),
        check_vma=False,
    )
```
